32 devices in a mesh: branch: 4 (over z), row: 4 (over y, x), col: 2 (over core).
Axes of the slice: x: 2, y: 2, z: 4, core: 2. Of those that a mesh axis runs over, the one named last changes fastest.
Arguments:
- alignment: bfloat16 [64, 128, 256], P(('branch', 'row'), 'col'), may hold values from -32 to 32
- pair_features: bfloat16 [128, 128, 128], P('col', 'row'), may hold values from -32 to 32
- w_row: bfloat16 [256, 1024], replicated, may hold values from -8 to 8
- row_output_weight: bfloat16 [256, 256], replicated, may hold values from -1.5 to 1.5
- w_bias: bfloat16 [128, 8], replicated, may hold values from -1 to 1
- w_column: bfloat16 [256, 1024], replicated, may hold values from -8 to 8
- column_output_weight: bfloat16 [256, 256], replicated, may hold values from -1.5 to 1.5
- outer_input_weight: bfloat16 [256, 64], replicated, may hold values from -0.375 to 0.375
- w_outer_out: bfloat16 [1024, 128], replicated, may hold values from -1.5 to 1.5
- w_triangle_in: bfloat16 [128, 512], replicated, may hold values from -0.5 to 0.5
- w_triangle_gate: bfloat16 [128, 128], replicated, may hold values from -0.5 to 0.5
- w_triangle_out: bfloat16 [128, 128], replicated, may hold values from -0.5 to 0.5
Outputs:
- alignment_out: bfloat16 [64, 128, 256], P(('branch', 'row'), 'col')
- pair_out: bfloat16 [128, 128, 128], P('col', 'row', 'branch')
The draws below stay inside these ranges and needn't reach their ends.
All inputs are finite; a program needn't handle non-finite values.
Results may differ from the reference program's by a relative error of at most 0.013.
Values may be sent and summed in bfloat16 or wider, within the bound.
A program may use at most 64 MiB of HBM per device.

```python
import math
import jax
import jax.numpy as jnp
from jax import lax

ALIGN_CHANNELS = 256
PAIR_WIDTH = 128
HEAD_COUNT = 8
HEAD_CHANNELS = 32
FACTOR_CHANNELS = 32
TRIANGLE_WIDTH = 128
SEQUENCE_COUNT = 64
RESIDUE_COUNT = 128


def scaled_field(key, array_shape):
    subkeys = jax.random.split(key, 3)
    base_values = jnp.clip(jax.random.normal(subkeys[0], array_shape, jnp.float32), -3.0, 3.0)
    row_scale = jnp.exp(jax.random.uniform(subkeys[1], array_shape[:-1] + (1,), jnp.float32, math.log(0.3), math.log(3.0)))
    channel_scale = jnp.exp(jax.random.uniform(subkeys[2], (array_shape[-1],), jnp.float32, math.log(0.3), math.log(3.0)))
    return base_values * row_scale * channel_scale


def attention_weight(key, random_tweak):
    weight_entries = jax.random.normal(jax.random.fold_in(key, random_tweak), (ALIGN_CHANNELS, 4 * ALIGN_CHANNELS), jnp.float32)
    weight_entries = jnp.clip(weight_entries, -5.0, 5.0) / math.sqrt(ALIGN_CHANNELS)
    return weight_entries


def draw_alignment(key, part):
    array_shape = (SEQUENCE_COUNT, RESIDUE_COUNT, ALIGN_CHANNELS)
    field_values = scaled_field(jax.random.fold_in(key, 101), array_shape)
    return field_values.astype(jnp.bfloat16)


def draw_pair_features(key, part):
    return scaled_field(jax.random.fold_in(key, 201), (RESIDUE_COUNT, RESIDUE_COUNT, PAIR_WIDTH)).astype(jnp.bfloat16)


def draw_w_row(key, part):
    return attention_weight(key, 301).astype(jnp.bfloat16)


def draw_w_column(key, part):
    return attention_weight(key, 401).astype(jnp.bfloat16)


def noise(key, dims, width, reach, kind=jnp.bfloat16):
    return jnp.clip(width * jax.random.normal(key, dims, jnp.float32), -reach, reach).astype(kind)


def setup_inputs(seed: int = 0) -> dict:
    keys = jax.random.split(jax.random.key(seed), 13)
    return {
        "alignment": draw_alignment(jax.random.fold_in(keys[12], 71), 0),
        "pair_features": draw_pair_features(jax.random.fold_in(keys[12], 71), 0),
        "w_row": draw_w_row(jax.random.fold_in(keys[12], 71), 0),
        "row_output_weight": noise(keys[3], (ALIGN_CHANNELS, ALIGN_CHANNELS), (ALIGN_CHANNELS // 16) ** -0.5, 1.5),
        "w_bias": noise(keys[4], (PAIR_WIDTH, HEAD_COUNT), (PAIR_WIDTH // 4) ** -0.5, 1.0),
        "w_column": draw_w_column(jax.random.fold_in(keys[12], 71), 0),
        "column_output_weight": noise(keys[6], (ALIGN_CHANNELS, ALIGN_CHANNELS), (ALIGN_CHANNELS // 16) ** -0.5, 1.5),
        "outer_input_weight": noise(keys[7], (ALIGN_CHANNELS, 2 * FACTOR_CHANNELS), ALIGN_CHANNELS ** -0.5, 0.375),
        "w_outer_out": noise(keys[8], (FACTOR_CHANNELS * FACTOR_CHANNELS, PAIR_WIDTH), (FACTOR_CHANNELS * FACTOR_CHANNELS // 64) ** -0.5, 1.5),
        "w_triangle_in": noise(keys[9], (PAIR_WIDTH, 4 * TRIANGLE_WIDTH), PAIR_WIDTH ** -0.5, 0.5),
        "w_triangle_gate": noise(keys[10], (PAIR_WIDTH, PAIR_WIDTH), PAIR_WIDTH ** -0.5, 0.5),
        "w_triangle_out": noise(keys[11], (TRIANGLE_WIDTH, PAIR_WIDTH), TRIANGLE_WIDTH ** -0.5, 0.5),
    }


EPSILON = 1e-05

def layer_norm(inputs):
    inputs = inputs.astype(jnp.float32)
    average = lax.optimization_barrier(jnp.mean(inputs, axis=-1, keepdims=True))
    variance = lax.optimization_barrier(jnp.mean(jnp.square(inputs - average), axis=-1, keepdims=True))
    return (inputs - average) * lax.rsqrt(variance + EPSILON)

def split_heads(row_entries):
    return row_entries.reshape(row_entries.shape[:-1] + (HEAD_COUNT, HEAD_CHANNELS))

def attend(query_matrix, key_matrix, value_matrix, head_bias):
    query_heads = split_heads(query_matrix.astype(jnp.float32))
    key_heads = split_heads(key_matrix.astype(jnp.float32))
    value_heads = split_heads(value_matrix.astype(jnp.float32))
    scores = jnp.einsum('bqhd,bkhd->bhqk', query_heads, key_heads)
    if head_bias is not None:
        scores = scores + head_bias.astype(jnp.float32)[None]
    attention = jax.nn.softmax(scores, axis=-1).astype(jnp.bfloat16)
    mixed_channels = jnp.einsum('bhqk,bkhd->bqhd', attention.astype(jnp.float32), value_heads)
    return mixed_channels.reshape(mixed_channels.shape[:2] + (ALIGN_CHANNELS,))

def gated_attention(row_entries, weight_matrix, output_weight, head_bias):
    normed_input = layer_norm(row_entries).astype(jnp.bfloat16)
    projected_input = jnp.dot(normed_input.reshape(-1, ALIGN_CHANNELS), weight_matrix, preferred_element_type=jnp.float32)
    projected_input = projected_input.reshape(row_entries.shape[:2] + (4 * ALIGN_CHANNELS,))
    query_matrix = (projected_input[..., :ALIGN_CHANNELS] * HEAD_CHANNELS ** (-0.5)).astype(jnp.bfloat16)
    key_matrix = projected_input[..., ALIGN_CHANNELS:2 * ALIGN_CHANNELS].astype(jnp.bfloat16)
    value_matrix = projected_input[..., 2 * ALIGN_CHANNELS:3 * ALIGN_CHANNELS].astype(jnp.bfloat16)
    gate_values = jax.nn.sigmoid(projected_input[..., 3 * ALIGN_CHANNELS:])
    attended = attend(query_matrix, key_matrix, value_matrix, head_bias)
    gated_output = (gate_values * attended).astype(jnp.bfloat16)
    residual_update = jnp.dot(gated_output.reshape(-1, ALIGN_CHANNELS), output_weight, preferred_element_type=jnp.float32)
    return (row_entries.astype(jnp.float32) + residual_update.reshape(row_entries.shape)).astype(jnp.bfloat16)

def reference(alignment, pair_features, w_row, row_output_weight, w_bias, w_column, column_output_weight, outer_input_weight, w_outer_out, w_triangle_in, w_triangle_gate, w_triangle_out):
    pair_normed = layer_norm(pair_features).astype(jnp.bfloat16)
    bias_flat = jnp.dot(pair_normed.reshape(-1, PAIR_WIDTH), w_bias, preferred_element_type=jnp.float32)
    head_bias = jnp.transpose(bias_flat.reshape(RESIDUE_COUNT, RESIDUE_COUNT, HEAD_COUNT), (2, 0, 1)).astype(jnp.bfloat16)

    def row_step(row_entries):
        return gated_attention(row_entries[None], w_row, row_output_weight, head_bias)[0]
    alignment_row = lax.map(row_step, alignment)

    def column_step(row_entries):
        return gated_attention(row_entries[None], w_column, column_output_weight, None)[0]
    by_residue = lax.map(column_step, jnp.transpose(alignment_row, (1, 0, 2)))
    alignment_out = jnp.transpose(by_residue, (1, 0, 2))
    outer_normed_input = layer_norm(alignment_out).astype(jnp.bfloat16)
    factor_pairs = jnp.dot(outer_normed_input.reshape(-1, ALIGN_CHANNELS), outer_input_weight, preferred_element_type=jnp.float32)
    factor_pairs = factor_pairs.reshape(SEQUENCE_COUNT, RESIDUE_COUNT, 2 * FACTOR_CHANNELS).astype(jnp.bfloat16)
    left_factor = factor_pairs[..., :FACTOR_CHANNELS]
    right_factor = factor_pairs[..., FACTOR_CHANNELS:].astype(jnp.float32)
    left_blocks = jnp.transpose(left_factor.reshape(SEQUENCE_COUNT, RESIDUE_COUNT // 32, 32, FACTOR_CHANNELS), (1, 0, 2, 3))

    def outer_block(block_rows):
        outer_sum = jnp.einsum('sic,sje->ijce', block_rows.astype(jnp.float32), right_factor) * (1.0 / SEQUENCE_COUNT)
        flat_rows = outer_sum.reshape(-1, FACTOR_CHANNELS * FACTOR_CHANNELS).astype(jnp.bfloat16)
        residual_update = jnp.dot(flat_rows, w_outer_out, preferred_element_type=jnp.float32)
        return residual_update.astype(jnp.bfloat16).reshape(32, RESIDUE_COUNT, PAIR_WIDTH)
    outer_update = lax.map(outer_block, left_blocks).reshape(RESIDUE_COUNT, RESIDUE_COUNT, PAIR_WIDTH)
    pair_mid = (pair_features.astype(jnp.float32) + outer_update.astype(jnp.float32)).astype(jnp.bfloat16)
    triangle_normed = layer_norm(pair_mid).astype(jnp.bfloat16)
    flat_normed = triangle_normed.reshape(-1, PAIR_WIDTH)
    projected_input = jnp.dot(flat_normed, w_triangle_in, preferred_element_type=jnp.float32)
    projected_input = projected_input.reshape(RESIDUE_COUNT, RESIDUE_COUNT, 4, TRIANGLE_WIDTH)
    tri_left = (jax.nn.sigmoid(projected_input[:, :, 1]) * projected_input[:, :, 0]).astype(jnp.bfloat16)
    tri_right = (jax.nn.sigmoid(projected_input[:, :, 3]) * projected_input[:, :, 2]).astype(jnp.bfloat16)
    triangle_sum = jnp.einsum('ikc,jkc->ijc', tri_left.astype(jnp.float32), tri_right.astype(jnp.float32)).astype(jnp.bfloat16)
    triangle_scaled = layer_norm(triangle_sum).astype(jnp.bfloat16)
    mixed_channels = jnp.dot(triangle_scaled.reshape(-1, TRIANGLE_WIDTH), w_triangle_out, preferred_element_type=jnp.float32)
    output_gate = jax.nn.sigmoid(jnp.dot(flat_normed, w_triangle_gate, preferred_element_type=jnp.float32))
    pair_out = (pair_mid.reshape(-1, PAIR_WIDTH).astype(jnp.float32) + output_gate * mixed_channels).astype(jnp.bfloat16)
    return (alignment_out, pair_out.reshape(RESIDUE_COUNT, RESIDUE_COUNT, PAIR_WIDTH))
```

```python
import functools

import jax
import jax.numpy as jnp
from jax import lax
from jax.experimental import pallas as pl
from jax.experimental.pallas import tpu as pltpu
from jax.sharding import PartitionSpec as P

ALIGN_CHANNELS = 256
PAIR_WIDTH = 128
HEAD_COUNT = 8
HEAD_CHANNELS = 32
FACTOR_CHANNELS = 32
TRIANGLE_WIDTH = 128


EPSILON = 1e-05


def layer_norm(inputs):
    inputs = inputs.astype(jnp.float32)
    average = jnp.mean(inputs, axis=-1, keepdims=True)
    variance = jnp.mean(jnp.square(inputs - average), axis=-1, keepdims=True)
    return (inputs - average) * lax.rsqrt(variance + EPSILON)


def project(normed_input, weight_matrix):
    flat_rows = normed_input.reshape(-1, normed_input.shape[-1])
    result = jnp.dot(flat_rows, weight_matrix, preferred_element_type=jnp.float32)
    return result.reshape(normed_input.shape[:-1] + (weight_matrix.shape[1],))


def split_heads(row_entries):
    return row_entries.reshape(row_entries.shape[:-1] + (HEAD_COUNT, HEAD_CHANNELS))


def attend(query_matrix, key_matrix, value_matrix, head_bias, seq_major):
    query_heads = split_heads(query_matrix)
    key_heads = split_heads(key_matrix)
    value_heads = split_heads(value_matrix)
    if seq_major:
        scores = jnp.einsum(
            "qbhd,kbhd->bhqk", query_heads, key_heads, preferred_element_type=jnp.float32
        )
    else:
        scores = jnp.einsum(
            "bqhd,bkhd->bhqk", query_heads, key_heads, preferred_element_type=jnp.float32
        )
    if head_bias is not None:
        scores = scores + head_bias.astype(jnp.float32)[None]
    attention = jax.nn.softmax(scores, axis=-1).astype(jnp.bfloat16)
    if seq_major:
        mixed_channels = jnp.einsum(
            "bhqk,kbhd->qbhd", attention, value_heads, preferred_element_type=jnp.float32
        )
    else:
        mixed_channels = jnp.einsum(
            "bhqk,bkhd->bqhd", attention, value_heads, preferred_element_type=jnp.float32
        )
    return mixed_channels.reshape(mixed_channels.shape[:2] + (ALIGN_CHANNELS,))


def column_attention(row_entries, weight_matrix, output_weight):
    normed_input = layer_norm(row_entries).astype(jnp.bfloat16)
    projected_input = project(normed_input, weight_matrix)
    query_matrix = (projected_input[..., :ALIGN_CHANNELS] * HEAD_CHANNELS ** (-0.5)).astype(
        jnp.bfloat16
    )
    key_matrix = projected_input[..., ALIGN_CHANNELS : 2 * ALIGN_CHANNELS].astype(jnp.bfloat16)
    value_matrix = projected_input[..., 2 * ALIGN_CHANNELS : 3 * ALIGN_CHANNELS].astype(
        jnp.bfloat16
    )
    gate_values = jax.nn.sigmoid(projected_input[..., 3 * ALIGN_CHANNELS :])
    attended = attend(query_matrix, key_matrix, value_matrix, None, True)
    gated_output = (gate_values * attended).astype(jnp.bfloat16)
    return (row_entries.astype(jnp.float32) + project(gated_output, output_weight)).astype(
        jnp.bfloat16
    )


def outer_mean(left_factor, right_factor, w_outer_out):
    seq_count = left_factor.shape[0]
    outer_sum = jnp.einsum(
        "sic,sje->ijce", left_factor, right_factor, preferred_element_type=jnp.float32
    ) * (1.0 / seq_count)
    flat_rows = outer_sum.reshape(-1, FACTOR_CHANNELS * FACTOR_CHANNELS).astype(jnp.bfloat16)
    residual_update = jnp.dot(flat_rows, w_outer_out, preferred_element_type=jnp.float32)
    return residual_update.reshape(outer_sum.shape[:2] + (PAIR_WIDTH,)).astype(jnp.bfloat16)

MESH = pl.DeviceIdType.MESH


def group_size(axes):
    size = 1
    for axis in axes:
        size *= lax.axis_size(axis)
    return size


def group_index(axes):
    index = 0
    for axis in axes:
        index = index * lax.axis_size(axis) + lax.axis_index(axis)
    return index


def group_device(axes, index):
    device = {}
    for axis in reversed(axes):
        size = lax.axis_size(axis)
        device[axis] = lax.rem(index, size)
        index = index // size
    return device


def each_peer(axes, action):
    size = group_size(axes)
    me = group_index(axes)

    def step(offset, carry):
        action(offset, lax.rem(me + offset, size), lax.rem(me + size - offset, size))
        return carry

    if size <= 16:
        for offset in range(1, size):
            step(offset, 0)
    else:
        lax.fori_loop(1, size, step, 0)


def greet(axes):
    barrier = pltpu.get_barrier_semaphore()
    each_peer(
        axes,
        lambda offset, to, source: pl.semaphore_signal(
            barrier, inc=1, device_id=group_device(axes, to), device_id_type=MESH
        ),
    )
    return group_size(axes) - 1


class Regular:
    def __init__(self, axes, scatter):
        self.axes, self.scatter = axes, scatter

    def semaphores(self):
        size = group_size(self.axes)
        return [pltpu.SemaphoreType.DMA((size,)), pltpu.SemaphoreType.DMA((size,))]

    def slots(self, x):
        return x if self.scatter else jax.ShapeDtypeStruct(
            (group_size(self.axes),) + x.shape, x.dtype
        )

    def greet(self):
        return greet(self.axes)

    def block(self, ref, index):
        return ref.at[index] if self.scatter else ref

    def copy(self, src, dst, sems, offset, to):
        return pltpu.make_async_remote_copy(
            src_ref=self.block(src, to),
            dst_ref=dst.at[group_index(self.axes)],
            send_sem=sems[0].at[offset],
            recv_sem=sems[1].at[offset],
            device_id=group_device(self.axes, to),
            device_id_type=MESH,
        )

    def own(self, src, dst, sems):
        me = group_index(self.axes)
        return pltpu.make_async_copy(self.block(src, me), dst.at[me], sems[1].at[0])

    def start(self, src, dst, sems):
        each_peer(
            self.axes,
            lambda offset, to, source: self.copy(src, dst, sems, offset, to).start(),
        )
        self.own(src, dst, sems).start()

    def wait(self, src, dst, sems):
        self.own(src, dst, sems).wait()

        def finish(offset, to, source):
            arriving = pltpu.make_async_remote_copy(
                src_ref=self.block(src, to),
                dst_ref=dst.at[source],
                send_sem=sems[0].at[offset],
                recv_sem=sems[1].at[offset],
                device_id=group_device(self.axes, to),
                device_id_type=MESH,
            )
            arriving.wait_send()
            arriving.wait_recv()

        each_peer(self.axes, finish)


class ColToRow:
    def __init__(self, split):
        self.split = split

    def sizes(self):
        rows, cols = lax.axis_size("row"), lax.axis_size("col")
        return rows, cols, rows // cols

    def sends(self):
        rows, cols, per = self.sizes()
        return lax.axis_size("branch") * cols if self.split else per * cols

    def receives(self):
        rows, cols, per = self.sizes()
        return lax.axis_size("branch") * rows // per if self.split else rows

    def semaphores(self):
        return [
            pltpu.SemaphoreType.DMA((self.sends(),)),
            pltpu.SemaphoreType.DMA((self.receives(),)),
            pltpu.SemaphoreType.DMA((1,)),
        ]

    def slots(self, x):
        shape = x.shape if self.split else x.shape[1:]
        return jax.ShapeDtypeStruct((self.receives(),) + shape, x.dtype)

    def target(self, k):
        rows, cols, per = self.sizes()
        branch, row, col = (lax.axis_index(a) for a in ("branch", "row", "col"))
        if self.split:
            group = branch * rows + row
            part = lax.axis_size("branch") * rows // per
            return k // cols, col * per + group // part, k % cols
        return branch, col * per + k // cols, k % cols

    def slot(self):
        rows, cols, per = self.sizes()
        if self.split:
            group = lax.axis_index("branch") * rows + lax.axis_index("row")
            return lax.rem(group, lax.axis_size("branch") * rows // per)
        return lax.axis_index("row")

    def origin(self, k):
        rows, cols, per = self.sizes()
        row = lax.axis_index("row")
        if self.split:
            part = lax.axis_size("branch") * rows // per
            group = lax.rem(row, per) * part + k
            return group // rows, lax.rem(group, rows), row // per
        return lax.axis_index("branch"), k, row // per

    def mine(self, device):
        same = device[0] == lax.axis_index("branch")
        same = jnp.logical_and(same, device[1] == lax.axis_index("row"))
        return jnp.logical_and(same, device[2] == lax.axis_index("col"))

    def loop(self, count, body):
        if count <= 16:
            for k in range(count):
                body(k)
        else:
            lax.fori_loop(0, count, lambda k, carry: (body(k), carry)[1], 0)

    def each(self, count, device_of, away, here=None):
        def body(k):
            device = device_of(k)
            mine = self.mine(device)
            pl.when(jnp.logical_not(mine))(lambda: away(k, device))
            if here is not None:
                pl.when(mine)(lambda: here(k))

        self.loop(count, body)

    def greet(self):
        barrier = pltpu.get_barrier_semaphore()

        def signal(k, device):
            pl.semaphore_signal(barrier, inc=1, device_id=device, device_id_type=MESH)

        self.each(self.sends(), self.target, signal)
        self.each(self.receives(), self.origin, signal)
        rows, cols, per = self.sizes()
        row = lax.axis_index("row")
        if self.split:
            part = lax.axis_size("branch") * rows // per
            aimed = lax.axis_index("col") * per + group_index(("branch", "row")) // part
            mine = (aimed == row).astype(jnp.int32)
        else:
            mine = (row // per == lax.axis_index("col")).astype(jnp.int32)
        return self.sends() + self.receives() - 2 * mine

    def block(self, src, k):
        if self.split:
            return src
        return src.at[k // self.sizes()[1]]

    def start(self, src, dst, sems):
        def away(k, device):
            pltpu.make_async_remote_copy(
                src_ref=self.block(src, k),
                dst_ref=dst.at[self.slot()],
                send_sem=sems[0].at[k],
                recv_sem=sems[1].at[self.slot()],
                device_id=device,
                device_id_type=MESH,
            ).start()

        def here(k):
            pltpu.make_async_copy(self.block(src, k), dst.at[self.slot()], sems[2].at[0]).start()

        self.each(self.sends(), self.target, away, here)

    def wait(self, src, dst, sems):
        def sent(k, device):
            pltpu.make_async_remote_copy(
                src_ref=self.block(src, k),
                dst_ref=dst.at[self.slot()],
                send_sem=sems[0].at[k],
                recv_sem=sems[1].at[self.slot()],
                device_id=device,
                device_id_type=MESH,
            ).wait_send()

        def here(k):
            pltpu.make_async_copy(self.block(src, k), dst.at[self.slot()], sems[2].at[0]).wait()

        def arrived(k, device):
            pltpu.make_async_remote_copy(
                src_ref=self.block(src, 0),
                dst_ref=dst.at[k],
                send_sem=sems[0].at[0],
                recv_sem=sems[1].at[k],
                device_id=device,
                device_id_type=MESH,
            ).wait_recv()

        self.each(self.sends(), self.target, sent, here)
        self.each(self.receives(), self.origin, arrived)


def exchange_kernel(moves, *refs):
    count = len(moves)
    sources, slots, rest = refs[:count], refs[count : 2 * count], list(refs[2 * count :])
    sems = []
    for move in moves:
        width = len(move.semaphores())
        sems.append(rest[:width])
        rest = rest[width:]
    total = 0
    for move in moves:
        total += move.greet()
    pl.semaphore_wait(pltpu.get_barrier_semaphore(), total)
    for move, source, slot, sem in zip(moves, sources, slots, sems):
        move.start(source, slot, sem)
    for move, source, slot, sem in zip(moves, sources, slots, sems):
        move.wait(source, slot, sem)


def exchange(collective_id, moves, arrays):
    scratch = []
    for move in moves:
        scratch += move.semaphores()
    slots = [move.slots(x) for move, x in zip(moves, arrays)]
    any_space = pl.BlockSpec(memory_space=pl.ANY)
    return pl.pallas_call(
        functools.partial(exchange_kernel, moves),
        out_shape=[jax.ShapeDtypeStruct(s.shape, s.dtype) for s in slots],
        in_specs=[any_space] * len(moves),
        out_specs=[any_space] * len(moves),
        scratch_shapes=scratch,
        compiler_params=pltpu.CompilerParams(
            collective_id=collective_id, has_side_effects=True
        ),
    )(*arrays)


def mix_kernel(sums_ref, weight_ref, out_ref, held, mixed, *sems):
    move = Regular(("branch",), True)
    pl.semaphore_wait(pltpu.get_barrier_semaphore(), move.greet())
    move.start(sums_ref, held, sems[:2])
    move.wait(sums_ref, held, sems[:2])
    sums = held[...].astype(jnp.float32).reshape(-1, held.shape[-1])
    average = jnp.mean(sums, axis=0, keepdims=True)
    centred = sums - average
    variance = jnp.mean(jnp.square(centred), axis=0, keepdims=True)
    scaled = (centred * lax.rsqrt(variance + EPSILON)).astype(jnp.bfloat16)
    product = lax.dot_general(
        weight_ref[...], scaled, (((0,), (0,)), ((), ())), preferred_element_type=jnp.float32
    )
    mixed[...] = product.reshape(mixed.shape).astype(mixed.dtype)
    move.start(mixed, out_ref, sems[2:])
    move.wait(mixed, out_ref, sems[2:])


def mix_channels(collective_id, sums, weight):
    move = Regular(("branch",), True)
    groups, _, width = sums.shape
    out = jax.ShapeDtypeStruct((groups, weight.shape[1] // groups, width), jnp.bfloat16)
    vmem = pl.BlockSpec(memory_space=pltpu.VMEM)
    return pl.pallas_call(
        mix_kernel,
        out_shape=out,
        in_specs=[vmem, vmem],
        out_specs=vmem,
        scratch_shapes=[
            pltpu.VMEM(sums.shape, sums.dtype),
            pltpu.VMEM(out.shape, out.dtype),
        ]
        + move.semaphores()
        + move.semaphores(),
        compiler_params=pltpu.CompilerParams(
            collective_id=collective_id, has_side_effects=True, vmem_limit_bytes=32 << 20
        ),
    )(sums, weight)


def local(
    alignment,
    pair_features,
    w_row,
    row_output_weight,
    w_bias,
    w_column,
    column_output_weight,
    outer_input_weight,
    w_outer_out,
    w_triangle_in,
    w_triangle_gate,
    w_triangle_out,
):
    rows = lax.axis_size("row")
    group_axes = ("branch", "row")
    groups_all = group_size(group_axes)
    seqs, residues, channels = alignment.shape
    tile_first, tile_second, _ = pair_features.shape
    pair_normed = layer_norm(pair_features).astype(jnp.bfloat16)
    bias_tile = jnp.einsum(
        "ijc,ch->hij", pair_normed, w_bias, preferred_element_type=jnp.float32
    ).astype(jnp.bfloat16)
    row_normed = layer_norm(alignment).astype(jnp.bfloat16)
    bias_slots, row_slots = exchange(
        0,
        [Regular(("row",), False), Regular(("col",), False)],
        [bias_tile.reshape(HEAD_COUNT, -1), row_normed],
    )
    head_bias = jnp.transpose(
        bias_slots.reshape(rows, HEAD_COUNT, tile_first, tile_second), (1, 2, 0, 3)
    ).reshape(HEAD_COUNT, tile_first, rows * tile_second)
    local_weight = jnp.concatenate(
        [w_row[:, :ALIGN_CHANNELS], w_row[:, 3 * ALIGN_CHANNELS :]], axis=1
    )
    local_projected = project(row_normed, local_weight)
    query_matrix = (local_projected[..., :ALIGN_CHANNELS] * HEAD_CHANNELS ** (-0.5)).astype(
        jnp.bfloat16
    )
    gate_values = jax.nn.sigmoid(local_projected[..., ALIGN_CHANNELS:])
    gathered = jnp.transpose(row_slots, (1, 0, 2, 3)).reshape(seqs, -1, channels)
    key_value = project(gathered, w_row[:, ALIGN_CHANNELS : 3 * ALIGN_CHANNELS]).astype(
        jnp.bfloat16
    )
    key_matrix = key_value[..., :ALIGN_CHANNELS]
    value_matrix = key_value[..., ALIGN_CHANNELS:]
    attended = attend(query_matrix, key_matrix, value_matrix, head_bias, False)
    row_gated = (gate_values * attended).astype(jnp.bfloat16)
    alignment_row = (alignment.astype(jnp.float32) + project(row_gated, row_output_weight)).astype(
        jnp.bfloat16
    )
    part = residues // groups_all
    outgoing = jnp.transpose(
        alignment_row.reshape(seqs, groups_all, part, channels), (1, 0, 2, 3)
    ).reshape(groups_all, seqs * part, channels)
    (columns,) = exchange(1, [Regular(group_axes, True)], [outgoing])
    columns = columns.reshape(groups_all * seqs, part, channels)
    column_new = column_attention(columns, w_column, column_output_weight)
    outer_normed_input = layer_norm(column_new).astype(jnp.bfloat16)
    factor_pairs = project(outer_normed_input, outer_input_weight).astype(jnp.bfloat16)
    all_seqs = groups_all * seqs
    back, left_slots, right_slots = exchange(
        2,
        [Regular(group_axes, True), Regular(group_axes, False), ColToRow(True)],
        [
            column_new.reshape(groups_all, seqs * part, channels),
            factor_pairs[..., :FACTOR_CHANNELS].reshape(all_seqs, part * FACTOR_CHANNELS),
            factor_pairs[..., FACTOR_CHANNELS:].reshape(all_seqs, part * FACTOR_CHANNELS),
        ],
    )
    alignment_out = jnp.transpose(
        back.reshape(groups_all, seqs, part, channels), (1, 0, 2, 3)
    ).reshape(seqs, residues, channels)
    left_factor = jnp.transpose(left_slots, (1, 0, 2)).reshape(
        all_seqs, residues, FACTOR_CHANNELS
    )
    right_factor = jnp.transpose(right_slots, (1, 0, 2)).reshape(
        all_seqs, tile_second, FACTOR_CHANNELS
    )
    outer_update = outer_mean(left_factor, right_factor, w_outer_out)
    pair_mid = (pair_features.astype(jnp.float32) + outer_update.astype(jnp.float32)).astype(
        jnp.bfloat16
    )
    groups = lax.axis_size("branch")
    branch_width = TRIANGLE_WIDTH // groups
    branch_start = lax.axis_index("branch") * branch_width
    out_width = PAIR_WIDTH // groups
    out_start = lax.axis_index("branch") * out_width
    triangle_normed = layer_norm(pair_mid).astype(jnp.bfloat16)
    flat_normed = triangle_normed.reshape(-1, PAIR_WIDTH)
    w_in = lax.dynamic_slice_in_dim(
        w_triangle_in.reshape(PAIR_WIDTH, 4, TRIANGLE_WIDTH), branch_start, branch_width, 2
    )
    gate_weight = lax.dynamic_slice_in_dim(w_triangle_gate, out_start, out_width, 1)
    w_all = jnp.concatenate([w_in.reshape(PAIR_WIDTH, 4 * branch_width), gate_weight], axis=1)
    projected = lax.dot_general(
        w_all, flat_normed, (((0,), (1,)), ((), ())), preferred_element_type=jnp.float32
    )
    tri = projected[: 4 * branch_width].reshape(4, branch_width, -1)
    tri_left = (jax.nn.sigmoid(tri[1]) * tri[0]).astype(jnp.bfloat16)
    tri_right = (jax.nn.sigmoid(tri[3]) * tri[2]).astype(jnp.bfloat16)
    output_gate = jax.nn.sigmoid(projected[4 * branch_width :])
    per = rows // lax.axis_size("col")
    right_parts = jnp.transpose(tri_right.reshape(branch_width, per, -1), (1, 0, 2))
    left_slots, right_slots = exchange(
        3, [Regular(("row",), False), ColToRow(False)], [tri_left, right_parts]
    )
    product = jnp.einsum(
        "rcik,rcjk->cij",
        left_slots.reshape(rows, branch_width, tile_first, tile_second),
        right_slots.reshape(rows, branch_width, tile_second, tile_second),
        preferred_element_type=jnp.float32,
    ).astype(jnp.bfloat16)
    sums = jnp.transpose(product.reshape(branch_width, groups, -1), (1, 0, 2))
    mixed = mix_channels(4, sums, w_triangle_out)
    mixed = jnp.transpose(mixed, (1, 0, 2)).reshape(out_width, -1)
    update = jnp.transpose(output_gate * mixed.astype(jnp.float32))
    pair_slice = lax.dynamic_slice_in_dim(pair_mid, out_start, out_width, 2).reshape(-1, out_width)
    pair_out = (pair_slice.astype(jnp.float32) + update).astype(jnp.bfloat16)
    return (alignment_out, pair_out.reshape(tile_first, tile_second, out_width))


def solution(mesh):
    in_specs = (
        P(("branch", "row"), "col", None),
        P("col", "row", None),
        P(),
        P(),
        P(),
        P(),
        P(),
        P(),
        P(),
        P(),
        P(),
        P(),
    )
    out_specs = (P(("branch", "row"), "col", None), P("col", "row", "branch"))
    return jax.shard_map(local, mesh=mesh, in_specs=in_specs, out_specs=out_specs, check_vma=False)
```

```python
import functools

import jax
import jax.numpy as jnp
import numpy as np
from jax import lax
from jax.experimental import pallas as pl
from jax.experimental.pallas import tpu as pltpu
from jax.sharding import PartitionSpec as P

ALIGN_CHANNELS = 256
PAIR_WIDTH = 128
HEAD_COUNT = 8
HEAD_CHANNELS = 32
FACTOR_CHANNELS = 32
TRIANGLE_WIDTH = 128


EPSILON = 1e-05


def layer_norm(inputs):
    inputs = inputs.astype(jnp.float32)
    average = jnp.mean(inputs, axis=-1, keepdims=True)
    variance = jnp.mean(jnp.square(inputs - average), axis=-1, keepdims=True)
    return (inputs - average) * lax.rsqrt(variance + EPSILON)


def project(normed_input, weight_matrix):
    flat_rows = normed_input.reshape(-1, normed_input.shape[-1])
    result = jnp.dot(flat_rows, weight_matrix, preferred_element_type=jnp.float32)
    return result.reshape(normed_input.shape[:-1] + (weight_matrix.shape[1],))


def split_heads(row_entries):
    return row_entries.reshape(row_entries.shape[:-1] + (HEAD_COUNT, HEAD_CHANNELS))


def attend(query_matrix, key_matrix, value_matrix, head_bias, seq_major):
    query_heads = split_heads(query_matrix)
    key_heads = split_heads(key_matrix)
    value_heads = split_heads(value_matrix)
    if seq_major:
        scores = jnp.einsum(
            "qbhd,kbhd->bhqk", query_heads, key_heads, preferred_element_type=jnp.float32
        )
    else:
        scores = jnp.einsum(
            "bqhd,bkhd->bhqk", query_heads, key_heads, preferred_element_type=jnp.float32
        )
    if head_bias is not None:
        scores = scores + head_bias.astype(jnp.float32)[None]
    attention = jax.nn.softmax(scores, axis=-1).astype(jnp.bfloat16)
    if seq_major:
        mixed_channels = jnp.einsum(
            "bhqk,kbhd->qbhd", attention, value_heads, preferred_element_type=jnp.float32
        )
    else:
        mixed_channels = jnp.einsum(
            "bhqk,bkhd->bqhd", attention, value_heads, preferred_element_type=jnp.float32
        )
    return mixed_channels.reshape(mixed_channels.shape[:2] + (ALIGN_CHANNELS,))


def column_attention(row_entries, weight_matrix, output_weight):
    normed_input = layer_norm(row_entries).astype(jnp.bfloat16)
    projected_input = project(normed_input, weight_matrix)
    query_matrix = (projected_input[..., :ALIGN_CHANNELS] * HEAD_CHANNELS ** (-0.5)).astype(
        jnp.bfloat16
    )
    key_matrix = projected_input[..., ALIGN_CHANNELS : 2 * ALIGN_CHANNELS].astype(jnp.bfloat16)
    value_matrix = projected_input[..., 2 * ALIGN_CHANNELS : 3 * ALIGN_CHANNELS].astype(
        jnp.bfloat16
    )
    gate_values = jax.nn.sigmoid(projected_input[..., 3 * ALIGN_CHANNELS :])
    attended = attend(query_matrix, key_matrix, value_matrix, None, True)
    gated_output = (gate_values * attended).astype(jnp.bfloat16)
    return (row_entries.astype(jnp.float32) + project(gated_output, output_weight)).astype(
        jnp.bfloat16
    )


def outer_mean(left_factor, right_factor, w_outer_out):
    seq_count = left_factor.shape[0]
    outer_sum = jnp.einsum(
        "sic,sje->ijce", left_factor, right_factor, preferred_element_type=jnp.float32
    ) * (1.0 / seq_count)
    flat_rows = outer_sum.reshape(-1, FACTOR_CHANNELS * FACTOR_CHANNELS).astype(jnp.bfloat16)
    residual_update = jnp.dot(flat_rows, w_outer_out, preferred_element_type=jnp.float32)
    return residual_update.reshape(outer_sum.shape[:2] + (PAIR_WIDTH,)).astype(jnp.bfloat16)

MESH = pl.DeviceIdType.MESH


def group_size(axes):
    size = 1
    for axis in axes:
        size *= lax.axis_size(axis)
    return size


def group_index(axes):
    index = 0
    for axis in axes:
        index = index * lax.axis_size(axis) + lax.axis_index(axis)
    return index


def group_device(axes, index):
    device = {}
    for axis in reversed(axes):
        size = lax.axis_size(axis)
        device[axis] = lax.rem(index, size)
        index = index // size
    return device


def each_peer(axes, action):
    size = group_size(axes)
    me = group_index(axes)

    def step(offset, carry):
        action(offset, lax.rem(me + offset, size), lax.rem(me + size - offset, size))
        return carry

    if size <= 16:
        for offset in range(1, size):
            step(offset, 0)
    else:
        lax.fori_loop(1, size, step, 0)


def greet(axes):
    barrier = pltpu.get_barrier_semaphore()
    each_peer(
        axes,
        lambda offset, to, source: pl.semaphore_signal(
            barrier, inc=1, device_id=group_device(axes, to), device_id_type=MESH
        ),
    )
    return group_size(axes) - 1


class Regular:
    def __init__(self, axes, scatter):
        self.axes, self.scatter = axes, scatter

    def semaphores(self):
        size = group_size(self.axes)
        return [pltpu.SemaphoreType.DMA((size,)), pltpu.SemaphoreType.DMA((size,))]

    def slots(self, x):
        return x if self.scatter else jax.ShapeDtypeStruct(
            (group_size(self.axes),) + x.shape, x.dtype
        )

    def greet(self):
        return greet(self.axes)

    def block(self, ref, index):
        return ref.at[index] if self.scatter else ref

    def copy(self, src, dst, sems, offset, to):
        return pltpu.make_async_remote_copy(
            src_ref=self.block(src, to),
            dst_ref=dst.at[group_index(self.axes)],
            send_sem=sems[0].at[offset],
            recv_sem=sems[1].at[offset],
            device_id=group_device(self.axes, to),
            device_id_type=MESH,
        )

    def own(self, src, dst, sems):
        me = group_index(self.axes)
        return pltpu.make_async_copy(self.block(src, me), dst.at[me], sems[1].at[0])

    def start(self, src, dst, sems):
        each_peer(
            self.axes,
            lambda offset, to, source: self.copy(src, dst, sems, offset, to).start(),
        )
        self.own(src, dst, sems).start()

    def wait(self, src, dst, sems):
        self.own(src, dst, sems).wait()

        def finish(offset, to, source):
            arriving = pltpu.make_async_remote_copy(
                src_ref=self.block(src, to),
                dst_ref=dst.at[source],
                send_sem=sems[0].at[offset],
                recv_sem=sems[1].at[offset],
                device_id=group_device(self.axes, to),
                device_id_type=MESH,
            )
            arriving.wait_send()
            arriving.wait_recv()

        each_peer(self.axes, finish)


class ColToRow:
    def __init__(self, split):
        self.split = split

    def sizes(self):
        rows, cols = lax.axis_size("row"), lax.axis_size("col")
        return rows, cols, rows // cols

    def sends(self):
        rows, cols, per = self.sizes()
        return lax.axis_size("branch") * cols if self.split else per * cols

    def receives(self):
        rows, cols, per = self.sizes()
        return lax.axis_size("branch") * rows // per if self.split else rows

    def semaphores(self):
        return [
            pltpu.SemaphoreType.DMA((self.sends(),)),
            pltpu.SemaphoreType.DMA((self.receives(),)),
            pltpu.SemaphoreType.DMA((1,)),
        ]

    def slots(self, x):
        shape = x.shape if self.split else x.shape[1:]
        return jax.ShapeDtypeStruct((self.receives(),) + shape, x.dtype)

    def target(self, k):
        rows, cols, per = self.sizes()
        branch, row, col = (lax.axis_index(a) for a in ("branch", "row", "col"))
        if self.split:
            group = branch * rows + row
            part = lax.axis_size("branch") * rows // per
            return k // cols, col * per + group // part, k % cols
        return branch, col * per + k // cols, k % cols

    def slot(self):
        rows, cols, per = self.sizes()
        if self.split:
            group = lax.axis_index("branch") * rows + lax.axis_index("row")
            return lax.rem(group, lax.axis_size("branch") * rows // per)
        return lax.axis_index("row")

    def origin(self, k):
        rows, cols, per = self.sizes()
        row = lax.axis_index("row")
        if self.split:
            part = lax.axis_size("branch") * rows // per
            group = lax.rem(row, per) * part + k
            return group // rows, lax.rem(group, rows), row // per
        return lax.axis_index("branch"), k, row // per

    def mine(self, device):
        same = device[0] == lax.axis_index("branch")
        same = jnp.logical_and(same, device[1] == lax.axis_index("row"))
        return jnp.logical_and(same, device[2] == lax.axis_index("col"))

    def loop(self, count, body):
        if count <= 16:
            for k in range(count):
                body(k)
        else:
            lax.fori_loop(0, count, lambda k, carry: (body(k), carry)[1], 0)

    def each(self, count, device_of, away, here=None):
        def body(k):
            device = device_of(k)
            mine = self.mine(device)
            pl.when(jnp.logical_not(mine))(lambda: away(k, device))
            if here is not None:
                pl.when(mine)(lambda: here(k))

        self.loop(count, body)

    def greet(self):
        barrier = pltpu.get_barrier_semaphore()

        def signal(k, device):
            pl.semaphore_signal(barrier, inc=1, device_id=device, device_id_type=MESH)

        self.each(self.sends(), self.target, signal)
        self.each(self.receives(), self.origin, signal)
        rows, cols, per = self.sizes()
        row = lax.axis_index("row")
        if self.split:
            part = lax.axis_size("branch") * rows // per
            aimed = lax.axis_index("col") * per + group_index(("branch", "row")) // part
            mine = (aimed == row).astype(jnp.int32)
        else:
            mine = (row // per == lax.axis_index("col")).astype(jnp.int32)
        return self.sends() + self.receives() - 2 * mine

    def block(self, src, k):
        if self.split:
            return src
        return src.at[k // self.sizes()[1]]

    def start(self, src, dst, sems):
        def away(k, device):
            pltpu.make_async_remote_copy(
                src_ref=self.block(src, k),
                dst_ref=dst.at[self.slot()],
                send_sem=sems[0].at[k],
                recv_sem=sems[1].at[self.slot()],
                device_id=device,
                device_id_type=MESH,
            ).start()

        def here(k):
            pltpu.make_async_copy(self.block(src, k), dst.at[self.slot()], sems[2].at[0]).start()

        self.each(self.sends(), self.target, away, here)

    def wait(self, src, dst, sems):
        def sent(k, device):
            pltpu.make_async_remote_copy(
                src_ref=self.block(src, k),
                dst_ref=dst.at[self.slot()],
                send_sem=sems[0].at[k],
                recv_sem=sems[1].at[self.slot()],
                device_id=device,
                device_id_type=MESH,
            ).wait_send()

        def here(k):
            pltpu.make_async_copy(self.block(src, k), dst.at[self.slot()], sems[2].at[0]).wait()

        def arrived(k, device):
            pltpu.make_async_remote_copy(
                src_ref=self.block(src, 0),
                dst_ref=dst.at[k],
                send_sem=sems[0].at[0],
                recv_sem=sems[1].at[k],
                device_id=device,
                device_id_type=MESH,
            ).wait_recv()

        self.each(self.sends(), self.target, sent, here)
        self.each(self.receives(), self.origin, arrived)


def exchange_kernel(moves, *refs):
    count = len(moves)
    sources, slots, rest = refs[:count], refs[count : 2 * count], list(refs[2 * count :])
    sems = []
    for move in moves:
        width = len(move.semaphores())
        sems.append(rest[:width])
        rest = rest[width:]
    total = 0
    for move in moves:
        total += move.greet()
    pl.semaphore_wait(pltpu.get_barrier_semaphore(), total)
    for move, source, slot, sem in zip(moves, sources, slots, sems):
        move.start(source, slot, sem)
    for move, source, slot, sem in zip(moves, sources, slots, sems):
        move.wait(source, slot, sem)


def exchange(collective_id, moves, arrays):
    scratch = []
    for move in moves:
        scratch += move.semaphores()
    slots = [move.slots(x) for move, x in zip(moves, arrays)]
    any_space = pl.BlockSpec(memory_space=pl.ANY)
    return pl.pallas_call(
        functools.partial(exchange_kernel, moves),
        out_shape=[jax.ShapeDtypeStruct(s.shape, s.dtype) for s in slots],
        in_specs=[any_space] * len(moves),
        out_specs=[any_space] * len(moves),
        scratch_shapes=scratch,
        compiler_params=pltpu.CompilerParams(
            collective_id=collective_id, has_side_effects=True
        ),
    )(*arrays)


def mix_kernel(sums_ref, weight_ref, out_ref, held, mixed, *sems):
    move = Regular(("branch",), True)
    pl.semaphore_wait(pltpu.get_barrier_semaphore(), move.greet())
    move.start(sums_ref, held, sems[:2])
    move.wait(sums_ref, held, sems[:2])
    sums = held[...].astype(jnp.float32).reshape(-1, held.shape[-1])
    average = jnp.mean(sums, axis=0, keepdims=True)
    centred = sums - average
    variance = jnp.mean(jnp.square(centred), axis=0, keepdims=True)
    scaled = (centred * lax.rsqrt(variance + EPSILON)).astype(jnp.bfloat16)
    product = lax.dot_general(
        weight_ref[...], scaled, (((0,), (0,)), ((), ())), preferred_element_type=jnp.float32
    )
    mixed[...] = product.reshape(mixed.shape).astype(mixed.dtype)
    move.start(mixed, out_ref, sems[2:])
    move.wait(mixed, out_ref, sems[2:])


def mix_channels(collective_id, sums, weight):
    move = Regular(("branch",), True)
    groups, _, width = sums.shape
    out = jax.ShapeDtypeStruct((groups, weight.shape[1] // groups, width), jnp.bfloat16)
    vmem = pl.BlockSpec(memory_space=pltpu.VMEM)
    return pl.pallas_call(
        mix_kernel,
        out_shape=out,
        in_specs=[vmem, vmem],
        out_specs=vmem,
        scratch_shapes=[
            pltpu.VMEM(sums.shape, sums.dtype),
            pltpu.VMEM(out.shape, out.dtype),
        ]
        + move.semaphores()
        + move.semaphores(),
        compiler_params=pltpu.CompilerParams(
            collective_id=collective_id, has_side_effects=True, vmem_limit_bytes=32 << 20
        ),
    )(sums, weight)


def softmax_down(scores):
    peak = jnp.max(scores, axis=0, keepdims=True)
    powers = jnp.exp(scores - peak)
    return (powers / jnp.sum(powers, axis=0, keepdims=True)).astype(jnp.bfloat16)


def dot(a, b, a_dim=1, b_dim=0):
    return lax.dot_general(
        a, b, (((a_dim,), (b_dim,)), ((), ())), preferred_element_type=jnp.float32
    )


def align_kernel(
    seqs,
    part,
    align_ref,
    bias_ref,
    w_row_ref,
    row_out_ref,
    w_col_ref,
    col_out_ref,
    w_left_ref,
    w_right_ref,
    permute_ref,
    same_ref,
    out_ref,
    left_slots,
    right_slots,
    normed,
    bias_slots,
    gathered,
    outgoing,
    columns,
    col_new,
    back,
    normed_cols,
    left,
    right,
    *sems,
):
    bf16, width = jnp.bfloat16, ALIGN_CHANNELS
    group_axes = ("branch", "row")
    groups = group_size(group_axes)
    over_row, over_col = Regular(("row",), False), Regular(("col",), False)
    swap, spread, aim = Regular(group_axes, True), Regular(group_axes, False), ColToRow(True)
    total = swap.greet() + over_col.greet() + aim.greet()
    pl.semaphore_wait(pltpu.get_barrier_semaphore(), total)
    over_row.start(bias_ref, bias_slots, sems[0:2])
    normed[...] = layer_norm(align_ref[...]).astype(bf16)
    over_col.start(normed, gathered, sems[2:4])
    residues = align_ref.shape[0] // seqs
    lanes = lax.broadcasted_iota(jnp.int32, (residues, width), 1)
    picks = [
        (lanes >= h * HEAD_CHANNELS) & (lanes < (h + 1) * HEAD_CHANNELS) for h in range(HEAD_COUNT)
    ]
    query = dot(normed[...], w_row_ref[:, :width]) * HEAD_CHANNELS ** (-0.5)
    gate = jax.nn.sigmoid(dot(normed[...], w_row_ref[:, 3 * width :]))
    over_col.wait(normed, gathered, sems[2:4])
    cols = gathered.shape[0]
    key_value = [
        dot(gathered[q], w_row_ref[:, width : 3 * width]).astype(bf16) for q in range(cols)
    ]
    over_row.wait(bias_ref, bias_slots, sems[0:2])
    bias = bias_slots[...].astype(jnp.float32).reshape(-1, bias_ref.shape[1])
    mixed = []
    for s in range(seqs):
        own = slice(s * residues, (s + 1) * residues)
        key = jnp.concatenate([kv[own, :width] for kv in key_value], axis=0)
        value = jnp.concatenate([kv[own, width:] for kv in key_value], axis=0)
        heads = jnp.concatenate([jnp.where(p, query[own], 0.0) for p in picks], axis=0)
        weights = softmax_down(dot(key, heads.astype(bf16), 1, 1) + bias)
        spreadout = dot(weights, value, 0, 0)
        attended = jnp.zeros((residues, width), jnp.float32)
        for h, p in enumerate(picks):
            attended = jnp.where(p, spreadout[h * residues : (h + 1) * residues], attended)
        mixed.append(attended)
    row_gated = (gate * jnp.concatenate(mixed, axis=0)).astype(bf16)
    updated = align_ref[...].astype(jnp.float32) + dot(row_gated, row_out_ref[...])
    outgoing[...] = dot(permute_ref[...], updated.astype(bf16)).astype(bf16).reshape(outgoing.shape)
    swap.start(outgoing, columns, sems[4:6])
    swap.wait(outgoing, columns, sems[4:6])
    entries = columns[...].reshape(-1, width)
    count = entries.shape[0]
    col_normed = layer_norm(entries).astype(bf16)
    projected = dot(col_normed, w_col_ref[...])
    query = projected[:, :width] * HEAD_CHANNELS ** (-0.5)
    key = projected[:, width : 2 * width].astype(bf16)
    value = projected[:, 2 * width : 3 * width].astype(bf16)
    gate = jax.nn.sigmoid(projected[:, 3 * width :])
    same = same_ref[...].astype(jnp.float32) > 0.5
    lanes = lax.broadcasted_iota(jnp.int32, (count, width), 1)
    attended = jnp.zeros((count, width), jnp.float32)
    for h in range(HEAD_COUNT):
        pick = (lanes >= h * HEAD_CHANNELS) & (lanes < (h + 1) * HEAD_CHANNELS)
        scores = dot(key, jnp.where(pick, query, 0.0).astype(bf16), 1, 1)
        weights = softmax_down(jnp.where(same, scores, jnp.finfo(jnp.float32).min))
        attended = jnp.where(pick, dot(weights, value, 0, 0), attended)
    col_gated = (gate * attended).astype(bf16)
    new = (entries.astype(jnp.float32) + dot(col_gated, col_out_ref[...])).astype(bf16)
    normed_new = layer_norm(new)
    for half in range(width // 128):
        normed_cols[half] = normed_new[:, half * 128 : (half + 1) * 128]
    all_seqs = count // part
    left_sum = right_sum = None
    for r in range(part):
        rows_r = jnp.concatenate(
            [normed_cols[half, pl.ds(r, all_seqs, stride=part), :] for half in range(width // 128)],
            axis=1,
        ).astype(bf16)
        left_r, right_r = dot(rows_r, w_left_ref[r]), dot(rows_r, w_right_ref[r])
        left_sum = left_r if r == 0 else left_sum + left_r
        right_sum = right_r if r == 0 else right_sum + right_r
    left[...] = left_sum.astype(bf16)
    right[...] = right_sum.astype(bf16)
    aim.start(right, right_slots, sems[10:13])
    spread.start(left, left_slots, sems[8:10])
    col_new[...] = new.reshape(col_new.shape)
    swap.start(col_new, back, sems[6:8])
    swap.wait(col_new, back, sems[6:8])
    result = dot(permute_ref[...], back[...].reshape(-1, width), 0, 0)
    out_ref[...] = result.astype(bf16)
    aim.wait(right, right_slots, sems[10:13])
    spread.wait(left, left_slots, sems[8:10])


def align_update(collective_id, alignment, bias, w_row, row_out, w_col, col_out, w_factor):
    bf16 = jnp.bfloat16
    seqs, residues, width = alignment.shape
    group_axes = ("branch", "row")
    groups = group_size(group_axes)
    part = residues // groups
    count = seqs * residues
    place = np.arange(count).reshape(seqs, groups, part).transpose(1, 0, 2).reshape(-1)
    permute = jnp.asarray(np.eye(count, dtype=np.float32)[place], bf16)
    rest = np.arange(count) % part
    same = jnp.asarray((rest[:, None] == rest[None, :]).astype(np.float32), bf16)
    eye = jnp.asarray(np.eye(part, dtype=np.float32), bf16)
    spread_out = lambda w: (eye[:, None, :, None] * w[None, :, None, :]).reshape(part, width, -1)
    w_left = spread_out(w_factor[:, :FACTOR_CHANNELS])
    w_right = spread_out(w_factor[:, FACTOR_CHANNELS:])
    over_row, over_col = Regular(("row",), False), Regular(("col",), False)
    swap, spread, aim = Regular(group_axes, True), Regular(group_axes, False), ColToRow(True)
    factor = jax.ShapeDtypeStruct((groups * seqs, part * FACTOR_CHANNELS), bf16)
    slots = (groups, seqs * part, width)
    scratch = [
        pltpu.VMEM((count, width), bf16),
        pltpu.VMEM((lax.axis_size("row"),) + bias.shape, bf16),
        pltpu.VMEM((lax.axis_size("col"), count, width), bf16),
        pltpu.VMEM(slots, bf16),
        pltpu.VMEM(slots, bf16),
        pltpu.VMEM(slots, bf16),
        pltpu.VMEM(slots, bf16),
        pltpu.VMEM((width // 128, count, 128), jnp.float32),
        pltpu.VMEM(factor.shape, bf16),
        pltpu.VMEM(factor.shape, bf16),
    ]
    for move in (over_row, over_col, swap, swap, spread, aim):
        scratch += move.semaphores()
    vmem = pl.BlockSpec(memory_space=pltpu.VMEM)
    anywhere = pl.BlockSpec(memory_space=pl.ANY)
    out, left_slots, right_slots = pl.pallas_call(
        functools.partial(align_kernel, seqs, part),
        out_shape=[
            jax.ShapeDtypeStruct((count, width), bf16),
            spread.slots(factor),
            aim.slots(factor),
        ],
        in_specs=[vmem] * 10,
        out_specs=[vmem, anywhere, anywhere],
        scratch_shapes=scratch,
        compiler_params=pltpu.CompilerParams(
            collective_id=collective_id, has_side_effects=True, vmem_limit_bytes=48 << 20
        ),
    )(
        alignment.reshape(count, width),
        bias,
        w_row,
        row_out,
        w_col,
        col_out,
        w_left,
        w_right,
        permute,
        same,
    )
    return out.reshape(alignment.shape), left_slots, right_slots


def align_unfused(
    alignment, pair_normed, w_row, row_output_weight, w_bias, w_column, column_output_weight,
    outer_input_weight,
):
    rows = lax.axis_size("row")
    group_axes = ("branch", "row")
    groups_all = group_size(group_axes)
    seqs, residues, channels = alignment.shape
    tile_first, tile_second, _ = pair_normed.shape
    bias_tile = jnp.einsum(
        "ijc,ch->hij", pair_normed, w_bias, preferred_element_type=jnp.float32
    ).astype(jnp.bfloat16)
    row_normed = layer_norm(alignment).astype(jnp.bfloat16)
    bias_slots, row_slots = exchange(
        0,
        [Regular(("row",), False), Regular(("col",), False)],
        [bias_tile.reshape(HEAD_COUNT, -1), row_normed],
    )
    head_bias = jnp.transpose(
        bias_slots.reshape(rows, HEAD_COUNT, tile_first, tile_second), (1, 2, 0, 3)
    ).reshape(HEAD_COUNT, tile_first, rows * tile_second)
    local_weight = jnp.concatenate(
        [w_row[:, :ALIGN_CHANNELS], w_row[:, 3 * ALIGN_CHANNELS :]], axis=1
    )
    local_projected = project(row_normed, local_weight)
    query_matrix = (local_projected[..., :ALIGN_CHANNELS] * HEAD_CHANNELS ** (-0.5)).astype(
        jnp.bfloat16
    )
    gate_values = jax.nn.sigmoid(local_projected[..., ALIGN_CHANNELS:])
    gathered = jnp.transpose(row_slots, (1, 0, 2, 3)).reshape(seqs, -1, channels)
    key_value = project(gathered, w_row[:, ALIGN_CHANNELS : 3 * ALIGN_CHANNELS]).astype(
        jnp.bfloat16
    )
    key_matrix = key_value[..., :ALIGN_CHANNELS]
    value_matrix = key_value[..., ALIGN_CHANNELS:]
    attended = attend(query_matrix, key_matrix, value_matrix, head_bias, False)
    row_gated = (gate_values * attended).astype(jnp.bfloat16)
    alignment_row = (alignment.astype(jnp.float32) + project(row_gated, row_output_weight)).astype(
        jnp.bfloat16
    )
    part = residues // groups_all
    outgoing = jnp.transpose(
        alignment_row.reshape(seqs, groups_all, part, channels), (1, 0, 2, 3)
    ).reshape(groups_all, seqs * part, channels)
    (columns,) = exchange(1, [Regular(group_axes, True)], [outgoing])
    columns = columns.reshape(groups_all * seqs, part, channels)
    column_new = column_attention(columns, w_column, column_output_weight)
    outer_normed_input = layer_norm(column_new).astype(jnp.bfloat16)
    factor_pairs = project(outer_normed_input, outer_input_weight).astype(jnp.bfloat16)
    all_seqs = groups_all * seqs
    back, left_slots, right_slots = exchange(
        2,
        [Regular(group_axes, True), Regular(group_axes, False), ColToRow(True)],
        [
            column_new.reshape(groups_all, seqs * part, channels),
            factor_pairs[..., :FACTOR_CHANNELS].reshape(all_seqs, part * FACTOR_CHANNELS),
            factor_pairs[..., FACTOR_CHANNELS:].reshape(all_seqs, part * FACTOR_CHANNELS),
        ],
    )
    alignment_out = jnp.transpose(
        back.reshape(groups_all, seqs, part, channels), (1, 0, 2, 3)
    ).reshape(seqs, residues, channels)
    return alignment_out, left_slots, right_slots


def local(
    alignment,
    pair_features,
    w_row,
    row_output_weight,
    w_bias,
    w_column,
    column_output_weight,
    outer_input_weight,
    w_outer_out,
    w_triangle_in,
    w_triangle_gate,
    w_triangle_out,
):
    rows = lax.axis_size("row")
    group_axes = ("branch", "row")
    groups_all = group_size(group_axes)
    seqs, residues, channels = alignment.shape
    tile_first, tile_second, _ = pair_features.shape
    pair_normed = layer_norm(pair_features).astype(jnp.bfloat16)
    if (seqs * residues // groups_all) % 16 == 0 and residues % 16 == 0:
        bias = jnp.einsum(
            "ijc,ch->jhi", pair_normed, w_bias, preferred_element_type=jnp.float32
        ).astype(jnp.bfloat16)
        alignment_out, left_slots, right_slots = align_update(
            5,
            alignment,
            bias.reshape(tile_second, -1),
            w_row,
            row_output_weight,
            w_column,
            column_output_weight,
            outer_input_weight,
        )
    else:
        alignment_out, left_slots, right_slots = align_unfused(
            alignment,
            pair_normed,
            w_row,
            row_output_weight,
            w_bias,
            w_column,
            column_output_weight,
            outer_input_weight,
        )
    all_seqs = groups_all * seqs
    left_factor = jnp.transpose(left_slots, (1, 0, 2)).reshape(
        all_seqs, residues, FACTOR_CHANNELS
    )
    right_factor = jnp.transpose(right_slots, (1, 0, 2)).reshape(
        all_seqs, tile_second, FACTOR_CHANNELS
    )
    outer_update = outer_mean(left_factor, right_factor, w_outer_out)
    pair_mid = (pair_features.astype(jnp.float32) + outer_update.astype(jnp.float32)).astype(
        jnp.bfloat16
    )
    groups = lax.axis_size("branch")
    branch_width = TRIANGLE_WIDTH // groups
    branch_start = lax.axis_index("branch") * branch_width
    out_width = PAIR_WIDTH // groups
    out_start = lax.axis_index("branch") * out_width
    triangle_normed = layer_norm(pair_mid).astype(jnp.bfloat16)
    flat_normed = triangle_normed.reshape(-1, PAIR_WIDTH)
    w_in = lax.dynamic_slice_in_dim(
        w_triangle_in.reshape(PAIR_WIDTH, 4, TRIANGLE_WIDTH), branch_start, branch_width, 2
    )
    gate_weight = lax.dynamic_slice_in_dim(w_triangle_gate, out_start, out_width, 1)
    w_all = jnp.concatenate([w_in.reshape(PAIR_WIDTH, 4 * branch_width), gate_weight], axis=1)
    projected = lax.dot_general(
        w_all, flat_normed, (((0,), (1,)), ((), ())), preferred_element_type=jnp.float32
    )
    tri = projected[: 4 * branch_width].reshape(4, branch_width, -1)
    tri_left = (jax.nn.sigmoid(tri[1]) * tri[0]).astype(jnp.bfloat16)
    tri_right = (jax.nn.sigmoid(tri[3]) * tri[2]).astype(jnp.bfloat16)
    output_gate = jax.nn.sigmoid(projected[4 * branch_width :])
    per = rows // lax.axis_size("col")
    right_parts = jnp.transpose(tri_right.reshape(branch_width, per, -1), (1, 0, 2))
    left_slots, right_slots = exchange(
        3, [Regular(("row",), False), ColToRow(False)], [tri_left, right_parts]
    )
    product = jnp.einsum(
        "rcik,rcjk->cij",
        left_slots.reshape(rows, branch_width, tile_first, tile_second),
        right_slots.reshape(rows, branch_width, tile_second, tile_second),
        preferred_element_type=jnp.float32,
    ).astype(jnp.bfloat16)
    sums = jnp.transpose(product.reshape(branch_width, groups, -1), (1, 0, 2))
    mixed = mix_channels(4, sums, w_triangle_out)
    mixed = jnp.transpose(mixed, (1, 0, 2)).reshape(out_width, -1)
    update = jnp.transpose(output_gate * mixed.astype(jnp.float32))
    pair_slice = lax.dynamic_slice_in_dim(pair_mid, out_start, out_width, 2).reshape(-1, out_width)
    pair_out = (pair_slice.astype(jnp.float32) + update).astype(jnp.bfloat16)
    return (alignment_out, pair_out.reshape(tile_first, tile_second, out_width))


def solution(mesh):
    in_specs = (
        P(("branch", "row"), "col", None),
        P("col", "row", None),
        P(),
        P(),
        P(),
        P(),
        P(),
        P(),
        P(),
        P(),
        P(),
        P(),
    )
    out_specs = (P(("branch", "row"), "col", None), P("col", "row", "branch"))
    return jax.shard_map(local, mesh=mesh, in_specs=in_specs, out_specs=out_specs, check_vma=False)
```

```python
import functools

import jax
import jax.numpy as jnp
import numpy as np
from jax import lax
from jax.experimental import pallas as pl
from jax.experimental.pallas import tpu as pltpu
from jax.sharding import PartitionSpec as P

ALIGN_CHANNELS = 256
PAIR_WIDTH = 128
HEAD_COUNT = 8
HEAD_CHANNELS = 32
FACTOR_CHANNELS = 32
TRIANGLE_WIDTH = 128


EPSILON = 1e-05


def layer_norm(inputs):
    inputs = inputs.astype(jnp.float32)
    average = jnp.mean(inputs, axis=-1, keepdims=True)
    variance = jnp.mean(jnp.square(inputs - average), axis=-1, keepdims=True)
    return (inputs - average) * lax.rsqrt(variance + EPSILON)


def project(normed_input, weight_matrix):
    flat_rows = normed_input.reshape(-1, normed_input.shape[-1])
    result = jnp.dot(flat_rows, weight_matrix, preferred_element_type=jnp.float32)
    return result.reshape(normed_input.shape[:-1] + (weight_matrix.shape[1],))


def split_heads(row_entries):
    return row_entries.reshape(row_entries.shape[:-1] + (HEAD_COUNT, HEAD_CHANNELS))


def attend(query_matrix, key_matrix, value_matrix, head_bias, seq_major):
    query_heads = split_heads(query_matrix)
    key_heads = split_heads(key_matrix)
    value_heads = split_heads(value_matrix)
    if seq_major:
        scores = jnp.einsum(
            "qbhd,kbhd->bhqk", query_heads, key_heads, preferred_element_type=jnp.float32
        )
    else:
        scores = jnp.einsum(
            "bqhd,bkhd->bhqk", query_heads, key_heads, preferred_element_type=jnp.float32
        )
    if head_bias is not None:
        scores = scores + head_bias.astype(jnp.float32)[None]
    attention = jax.nn.softmax(scores, axis=-1).astype(jnp.bfloat16)
    if seq_major:
        mixed_channels = jnp.einsum(
            "bhqk,kbhd->qbhd", attention, value_heads, preferred_element_type=jnp.float32
        )
    else:
        mixed_channels = jnp.einsum(
            "bhqk,bkhd->bqhd", attention, value_heads, preferred_element_type=jnp.float32
        )
    return mixed_channels.reshape(mixed_channels.shape[:2] + (ALIGN_CHANNELS,))


def column_attention(row_entries, weight_matrix, output_weight):
    normed_input = layer_norm(row_entries).astype(jnp.bfloat16)
    projected_input = project(normed_input, weight_matrix)
    query_matrix = (projected_input[..., :ALIGN_CHANNELS] * HEAD_CHANNELS ** (-0.5)).astype(
        jnp.bfloat16
    )
    key_matrix = projected_input[..., ALIGN_CHANNELS : 2 * ALIGN_CHANNELS].astype(jnp.bfloat16)
    value_matrix = projected_input[..., 2 * ALIGN_CHANNELS : 3 * ALIGN_CHANNELS].astype(
        jnp.bfloat16
    )
    gate_values = jax.nn.sigmoid(projected_input[..., 3 * ALIGN_CHANNELS :])
    attended = attend(query_matrix, key_matrix, value_matrix, None, True)
    gated_output = (gate_values * attended).astype(jnp.bfloat16)
    return (row_entries.astype(jnp.float32) + project(gated_output, output_weight)).astype(
        jnp.bfloat16
    )


def outer_mean(left_factor, right_factor, w_outer_out):
    seq_count = left_factor.shape[0]
    outer_sum = jnp.einsum(
        "sic,sje->ijce", left_factor, right_factor, preferred_element_type=jnp.float32
    ) * (1.0 / seq_count)
    flat_rows = outer_sum.reshape(-1, FACTOR_CHANNELS * FACTOR_CHANNELS).astype(jnp.bfloat16)
    residual_update = jnp.dot(flat_rows, w_outer_out, preferred_element_type=jnp.float32)
    return residual_update.reshape(outer_sum.shape[:2] + (PAIR_WIDTH,)).astype(jnp.bfloat16)

MESH = pl.DeviceIdType.MESH


def group_size(axes):
    size = 1
    for axis in axes:
        size *= lax.axis_size(axis)
    return size


def group_index(axes):
    index = 0
    for axis in axes:
        index = index * lax.axis_size(axis) + lax.axis_index(axis)
    return index


def group_device(axes, index):
    device = {}
    for axis in reversed(axes):
        size = lax.axis_size(axis)
        device[axis] = lax.rem(index, size)
        index = index // size
    return device


def each_peer(axes, action):
    size = group_size(axes)
    me = group_index(axes)

    def step(offset, carry):
        action(offset, lax.rem(me + offset, size), lax.rem(me + size - offset, size))
        return carry

    if size <= 16:
        for offset in range(1, size):
            step(offset, 0)
    else:
        lax.fori_loop(1, size, step, 0)


def greet(axes):
    barrier = pltpu.get_barrier_semaphore()
    each_peer(
        axes,
        lambda offset, to, source: pl.semaphore_signal(
            barrier, inc=1, device_id=group_device(axes, to), device_id_type=MESH
        ),
    )
    return group_size(axes) - 1


class Regular:
    def __init__(self, axes, scatter):
        self.axes, self.scatter = axes, scatter

    def semaphores(self):
        size = group_size(self.axes)
        return [pltpu.SemaphoreType.DMA((size,)), pltpu.SemaphoreType.DMA((size,))]

    def slots(self, x):
        return x if self.scatter else jax.ShapeDtypeStruct(
            (group_size(self.axes),) + x.shape, x.dtype
        )

    def greet(self):
        return greet(self.axes)

    def block(self, ref, index):
        return ref.at[index] if self.scatter else ref

    def copy(self, src, dst, sems, offset, to):
        return pltpu.make_async_remote_copy(
            src_ref=self.block(src, to),
            dst_ref=dst.at[group_index(self.axes)],
            send_sem=sems[0].at[offset],
            recv_sem=sems[1].at[offset],
            device_id=group_device(self.axes, to),
            device_id_type=MESH,
        )

    def own(self, src, dst, sems):
        me = group_index(self.axes)
        return pltpu.make_async_copy(self.block(src, me), dst.at[me], sems[1].at[0])

    def start(self, src, dst, sems):
        each_peer(
            self.axes,
            lambda offset, to, source: self.copy(src, dst, sems, offset, to).start(),
        )
        self.own(src, dst, sems).start()

    def wait(self, src, dst, sems):
        self.own(src, dst, sems).wait()

        def finish(offset, to, source):
            arriving = pltpu.make_async_remote_copy(
                src_ref=self.block(src, to),
                dst_ref=dst.at[source],
                send_sem=sems[0].at[offset],
                recv_sem=sems[1].at[offset],
                device_id=group_device(self.axes, to),
                device_id_type=MESH,
            )
            arriving.wait_send()
            arriving.wait_recv()

        each_peer(self.axes, finish)


class ColToRow:
    def __init__(self, split):
        self.split = split

    def sizes(self):
        rows, cols = lax.axis_size("row"), lax.axis_size("col")
        return rows, cols, rows // cols

    def sends(self):
        rows, cols, per = self.sizes()
        return lax.axis_size("branch") * cols if self.split else per * cols

    def receives(self):
        rows, cols, per = self.sizes()
        return lax.axis_size("branch") * rows // per if self.split else rows

    def semaphores(self):
        return [
            pltpu.SemaphoreType.DMA((self.sends(),)),
            pltpu.SemaphoreType.DMA((self.receives(),)),
            pltpu.SemaphoreType.DMA((1,)),
        ]

    def slots(self, x):
        shape = x.shape if self.split else x.shape[1:]
        return jax.ShapeDtypeStruct((self.receives(),) + shape, x.dtype)

    def target(self, k):
        rows, cols, per = self.sizes()
        branch, row, col = (lax.axis_index(a) for a in ("branch", "row", "col"))
        if self.split:
            group = branch * rows + row
            part = lax.axis_size("branch") * rows // per
            return k // cols, col * per + group // part, k % cols
        return branch, col * per + k // cols, k % cols

    def slot(self):
        rows, cols, per = self.sizes()
        if self.split:
            group = lax.axis_index("branch") * rows + lax.axis_index("row")
            return lax.rem(group, lax.axis_size("branch") * rows // per)
        return lax.axis_index("row")

    def origin(self, k):
        rows, cols, per = self.sizes()
        row = lax.axis_index("row")
        if self.split:
            part = lax.axis_size("branch") * rows // per
            group = lax.rem(row, per) * part + k
            return group // rows, lax.rem(group, rows), row // per
        return lax.axis_index("branch"), k, row // per

    def mine(self, device):
        same = device[0] == lax.axis_index("branch")
        same = jnp.logical_and(same, device[1] == lax.axis_index("row"))
        return jnp.logical_and(same, device[2] == lax.axis_index("col"))

    def loop(self, count, body):
        if count <= 16:
            for k in range(count):
                body(k)
        else:
            lax.fori_loop(0, count, lambda k, carry: (body(k), carry)[1], 0)

    def each(self, count, device_of, away, here=None):
        def body(k):
            device = device_of(k)
            mine = self.mine(device)
            pl.when(jnp.logical_not(mine))(lambda: away(k, device))
            if here is not None:
                pl.when(mine)(lambda: here(k))

        self.loop(count, body)

    def greet(self):
        barrier = pltpu.get_barrier_semaphore()

        def signal(k, device):
            pl.semaphore_signal(barrier, inc=1, device_id=device, device_id_type=MESH)

        self.each(self.sends(), self.target, signal)
        self.each(self.receives(), self.origin, signal)
        rows, cols, per = self.sizes()
        row = lax.axis_index("row")
        if self.split:
            part = lax.axis_size("branch") * rows // per
            aimed = lax.axis_index("col") * per + group_index(("branch", "row")) // part
            mine = (aimed == row).astype(jnp.int32)
        else:
            mine = (row // per == lax.axis_index("col")).astype(jnp.int32)
        return self.sends() + self.receives() - 2 * mine

    def block(self, src, k):
        if self.split:
            return src
        return src.at[k // self.sizes()[1]]

    def start(self, src, dst, sems):
        def away(k, device):
            pltpu.make_async_remote_copy(
                src_ref=self.block(src, k),
                dst_ref=dst.at[self.slot()],
                send_sem=sems[0].at[k],
                recv_sem=sems[1].at[self.slot()],
                device_id=device,
                device_id_type=MESH,
            ).start()

        def here(k):
            pltpu.make_async_copy(self.block(src, k), dst.at[self.slot()], sems[2].at[0]).start()

        self.each(self.sends(), self.target, away, here)

    def wait(self, src, dst, sems):
        def sent(k, device):
            pltpu.make_async_remote_copy(
                src_ref=self.block(src, k),
                dst_ref=dst.at[self.slot()],
                send_sem=sems[0].at[k],
                recv_sem=sems[1].at[self.slot()],
                device_id=device,
                device_id_type=MESH,
            ).wait_send()

        def here(k):
            pltpu.make_async_copy(self.block(src, k), dst.at[self.slot()], sems[2].at[0]).wait()

        def arrived(k, device):
            pltpu.make_async_remote_copy(
                src_ref=self.block(src, 0),
                dst_ref=dst.at[k],
                send_sem=sems[0].at[0],
                recv_sem=sems[1].at[k],
                device_id=device,
                device_id_type=MESH,
            ).wait_recv()

        self.each(self.sends(), self.target, sent, here)
        self.each(self.receives(), self.origin, arrived)


def exchange_kernel(moves, *refs):
    count = len(moves)
    sources, slots, rest = refs[:count], refs[count : 2 * count], list(refs[2 * count :])
    sems = []
    for move in moves:
        width = len(move.semaphores())
        sems.append(rest[:width])
        rest = rest[width:]
    total = 0
    for move in moves:
        total += move.greet()
    pl.semaphore_wait(pltpu.get_barrier_semaphore(), total)
    for move, source, slot, sem in zip(moves, sources, slots, sems):
        move.start(source, slot, sem)
    for move, source, slot, sem in zip(moves, sources, slots, sems):
        move.wait(source, slot, sem)


def exchange(collective_id, moves, arrays):
    scratch = []
    for move in moves:
        scratch += move.semaphores()
    slots = [move.slots(x) for move, x in zip(moves, arrays)]
    any_space = pl.BlockSpec(memory_space=pl.ANY)
    return pl.pallas_call(
        functools.partial(exchange_kernel, moves),
        out_shape=[jax.ShapeDtypeStruct(s.shape, s.dtype) for s in slots],
        in_specs=[any_space] * len(moves),
        out_specs=[any_space] * len(moves),
        scratch_shapes=scratch,
        compiler_params=pltpu.CompilerParams(
            collective_id=collective_id, has_side_effects=True
        ),
    )(*arrays)


def mix_kernel(sums_ref, weight_ref, out_ref, held, mixed, *sems):
    move = Regular(("branch",), True)
    pl.semaphore_wait(pltpu.get_barrier_semaphore(), move.greet())
    move.start(sums_ref, held, sems[:2])
    move.wait(sums_ref, held, sems[:2])
    sums = held[...].astype(jnp.float32).reshape(-1, held.shape[-1])
    average = jnp.mean(sums, axis=0, keepdims=True)
    centred = sums - average
    variance = jnp.mean(jnp.square(centred), axis=0, keepdims=True)
    scaled = (centred * lax.rsqrt(variance + EPSILON)).astype(jnp.bfloat16)
    product = lax.dot_general(
        weight_ref[...], scaled, (((0,), (0,)), ((), ())), preferred_element_type=jnp.float32
    )
    mixed[...] = product.reshape(mixed.shape).astype(mixed.dtype)
    move.start(mixed, out_ref, sems[2:])
    move.wait(mixed, out_ref, sems[2:])


def mix_channels(collective_id, sums, weight):
    move = Regular(("branch",), True)
    groups, _, width = sums.shape
    out = jax.ShapeDtypeStruct((groups, weight.shape[1] // groups, width), jnp.bfloat16)
    vmem = pl.BlockSpec(memory_space=pltpu.VMEM)
    return pl.pallas_call(
        mix_kernel,
        out_shape=out,
        in_specs=[vmem, vmem],
        out_specs=vmem,
        scratch_shapes=[
            pltpu.VMEM(sums.shape, sums.dtype),
            pltpu.VMEM(out.shape, out.dtype),
        ]
        + move.semaphores()
        + move.semaphores(),
        compiler_params=pltpu.CompilerParams(
            collective_id=collective_id, has_side_effects=True, vmem_limit_bytes=32 << 20
        ),
    )(sums, weight)


def softmax_down(scores):
    peak = jnp.max(scores, axis=0, keepdims=True)
    powers = jnp.exp(scores - peak)
    return (powers / jnp.sum(powers, axis=0, keepdims=True)).astype(jnp.bfloat16)


def dot(a, b, a_dim=1, b_dim=0):
    return lax.dot_general(
        a, b, (((a_dim,), (b_dim,)), ((), ())), preferred_element_type=jnp.float32
    )


def align_kernel(
    seqs,
    part,
    align_ref,
    bias_ref,
    w_row_ref,
    row_out_ref,
    w_col_ref,
    col_out_ref,
    w_left_ref,
    w_right_ref,
    permute_ref,
    same_ref,
    out_ref,
    left_slots,
    right_slots,
    normed,
    bias_slots,
    gathered,
    outgoing,
    columns,
    col_new,
    back,
    normed_cols,
    left,
    right,
    *sems,
):
    bf16, width = jnp.bfloat16, ALIGN_CHANNELS
    group_axes = ("branch", "row")
    groups = group_size(group_axes)
    over_row, over_col = Regular(("row",), False), Regular(("col",), False)
    swap, spread, aim = Regular(group_axes, True), Regular(group_axes, False), ColToRow(True)
    total = swap.greet() + over_col.greet() + aim.greet()
    pl.semaphore_wait(pltpu.get_barrier_semaphore(), total)
    over_row.start(bias_ref, bias_slots, sems[0:2])
    normed[...] = layer_norm(align_ref[...]).astype(bf16)
    over_col.start(normed, gathered, sems[2:4])
    residues = align_ref.shape[0] // seqs
    lanes = lax.broadcasted_iota(jnp.int32, (residues, width), 1)
    picks = [
        (lanes >= h * HEAD_CHANNELS) & (lanes < (h + 1) * HEAD_CHANNELS) for h in range(HEAD_COUNT)
    ]
    query = dot(normed[...], w_row_ref[:, :width]) * HEAD_CHANNELS ** (-0.5)
    gate = jax.nn.sigmoid(dot(normed[...], w_row_ref[:, 3 * width :]))
    over_col.wait(normed, gathered, sems[2:4])
    cols = gathered.shape[0]
    key_value = [
        dot(gathered[q], w_row_ref[:, width : 3 * width]).astype(bf16) for q in range(cols)
    ]
    over_row.wait(bias_ref, bias_slots, sems[0:2])
    bias = bias_slots[...].astype(jnp.float32).reshape(-1, bias_ref.shape[1])
    mixed = []
    for s in range(seqs):
        own = slice(s * residues, (s + 1) * residues)
        key = jnp.concatenate([kv[own, :width] for kv in key_value], axis=0)
        value = jnp.concatenate([kv[own, width:] for kv in key_value], axis=0)
        heads = jnp.concatenate([jnp.where(p, query[own], 0.0) for p in picks], axis=0)
        weights = softmax_down(dot(key, heads.astype(bf16), 1, 1) + bias)
        spreadout = dot(weights, value, 0, 0)
        attended = jnp.zeros((residues, width), jnp.float32)
        for h, p in enumerate(picks):
            attended = jnp.where(p, spreadout[h * residues : (h + 1) * residues], attended)
        mixed.append(attended)
    row_gated = (gate * jnp.concatenate(mixed, axis=0)).astype(bf16)
    updated = align_ref[...].astype(jnp.float32) + dot(row_gated, row_out_ref[...])
    outgoing[...] = dot(permute_ref[...], updated.astype(bf16)).astype(bf16).reshape(outgoing.shape)
    swap.start(outgoing, columns, sems[4:6])
    swap.wait(outgoing, columns, sems[4:6])
    entries = columns[...].reshape(-1, width)
    count = entries.shape[0]
    col_normed = layer_norm(entries).astype(bf16)
    projected = dot(col_normed, w_col_ref[...])
    query = projected[:, :width] * HEAD_CHANNELS ** (-0.5)
    key = projected[:, width : 2 * width].astype(bf16)
    value = projected[:, 2 * width : 3 * width].astype(bf16)
    gate = jax.nn.sigmoid(projected[:, 3 * width :])
    same = same_ref[...].astype(jnp.float32) > 0.5
    lanes = lax.broadcasted_iota(jnp.int32, (count, width), 1)
    attended = jnp.zeros((count, width), jnp.float32)
    for h in range(HEAD_COUNT):
        pick = (lanes >= h * HEAD_CHANNELS) & (lanes < (h + 1) * HEAD_CHANNELS)
        scores = dot(key, jnp.where(pick, query, 0.0).astype(bf16), 1, 1)
        weights = softmax_down(jnp.where(same, scores, jnp.finfo(jnp.float32).min))
        attended = jnp.where(pick, dot(weights, value, 0, 0), attended)
    col_gated = (gate * attended).astype(bf16)
    new = (entries.astype(jnp.float32) + dot(col_gated, col_out_ref[...])).astype(bf16)
    normed_new = layer_norm(new)
    for half in range(width // 128):
        normed_cols[half] = normed_new[:, half * 128 : (half + 1) * 128]
    all_seqs = count // part
    left_sum = right_sum = None
    for r in range(part):
        rows_r = jnp.concatenate(
            [normed_cols[half, pl.ds(r, all_seqs, stride=part), :] for half in range(width // 128)],
            axis=1,
        ).astype(bf16)
        left_r, right_r = dot(rows_r, w_left_ref[r]), dot(rows_r, w_right_ref[r])
        left_sum = left_r if r == 0 else left_sum + left_r
        right_sum = right_r if r == 0 else right_sum + right_r
    left[...] = left_sum.astype(bf16)
    right[...] = right_sum.astype(bf16)
    aim.start(right, right_slots, sems[10:13])
    spread.start(left, left_slots, sems[8:10])
    col_new[...] = new.reshape(col_new.shape)
    swap.start(col_new, back, sems[6:8])
    swap.wait(col_new, back, sems[6:8])
    result = dot(permute_ref[...], back[...].reshape(-1, width), 0, 0)
    out_ref[...] = result.astype(bf16)
    aim.wait(right, right_slots, sems[10:13])
    spread.wait(left, left_slots, sems[8:10])


def align_update(collective_id, alignment, bias, w_row, row_out, w_col, col_out, w_factor):
    bf16 = jnp.bfloat16
    seqs, residues, width = alignment.shape
    group_axes = ("branch", "row")
    groups = group_size(group_axes)
    part = residues // groups
    count = seqs * residues
    place = np.arange(count).reshape(seqs, groups, part).transpose(1, 0, 2).reshape(-1)
    permute = jnp.asarray(np.eye(count, dtype=np.float32)[place], bf16)
    rest = np.arange(count) % part
    same = jnp.asarray((rest[:, None] == rest[None, :]).astype(np.float32), bf16)
    eye = jnp.asarray(np.eye(part, dtype=np.float32), bf16)
    spread_out = lambda w: (eye[:, None, :, None] * w[None, :, None, :]).reshape(part, width, -1)
    w_left = spread_out(w_factor[:, :FACTOR_CHANNELS])
    w_right = spread_out(w_factor[:, FACTOR_CHANNELS:])
    over_row, over_col = Regular(("row",), False), Regular(("col",), False)
    swap, spread, aim = Regular(group_axes, True), Regular(group_axes, False), ColToRow(True)
    factor = jax.ShapeDtypeStruct((groups * seqs, part * FACTOR_CHANNELS), bf16)
    slots = (groups, seqs * part, width)
    scratch = [
        pltpu.VMEM((count, width), bf16),
        pltpu.VMEM((lax.axis_size("row"),) + bias.shape, bf16),
        pltpu.VMEM((lax.axis_size("col"), count, width), bf16),
        pltpu.VMEM(slots, bf16),
        pltpu.VMEM(slots, bf16),
        pltpu.VMEM(slots, bf16),
        pltpu.VMEM(slots, bf16),
        pltpu.VMEM((width // 128, count, 128), jnp.float32),
        pltpu.VMEM(factor.shape, bf16),
        pltpu.VMEM(factor.shape, bf16),
    ]
    for move in (over_row, over_col, swap, swap, spread, aim):
        scratch += move.semaphores()
    vmem = pl.BlockSpec(memory_space=pltpu.VMEM)
    anywhere = pl.BlockSpec(memory_space=pl.ANY)
    out, left_slots, right_slots = pl.pallas_call(
        functools.partial(align_kernel, seqs, part),
        out_shape=[
            jax.ShapeDtypeStruct((count, width), bf16),
            spread.slots(factor),
            aim.slots(factor),
        ],
        in_specs=[vmem] * 10,
        out_specs=[vmem, anywhere, anywhere],
        scratch_shapes=scratch,
        compiler_params=pltpu.CompilerParams(
            collective_id=collective_id, has_side_effects=True, vmem_limit_bytes=48 << 20
        ),
    )(
        alignment.reshape(count, width),
        bias,
        w_row,
        row_out,
        w_col,
        col_out,
        w_left,
        w_right,
        permute,
        same,
    )
    return out.reshape(alignment.shape), left_slots, right_slots


def triangle_kernel(width, left_ref, right_ref, out_ref, left_slots, right_slots, *sems):
    over_row, aim = Regular(("row",), False), ColToRow(False)
    total = over_row.greet() + aim.greet()
    pl.semaphore_wait(pltpu.get_barrier_semaphore(), total)
    over_row.start(left_ref, left_slots, sems[0:2])
    aim.start(right_ref, right_slots, sems[2:5])
    over_row.wait(left_ref, left_slots, sems[0:2])
    aim.wait(right_ref, right_slots, sems[2:5])
    left = left_slots[...].reshape(-1, left_ref.shape[-1])
    right = right_slots[...].reshape(-1, right_ref.shape[-1])
    first, second = left.shape[1] // width, right.shape[1] // width
    batch = max(1, 128 // min(first, second))
    for start in range(0, width, batch):
        product = dot(
            left[:, start * first : (start + batch) * first],
            right[:, start * second : (start + batch) * second],
            0,
            0,
        )
        for c in range(batch):
            out_ref[start + c] = product[
                c * first : (c + 1) * first, c * second : (c + 1) * second
            ].astype(out_ref.dtype)


def triangle_product(collective_id, left, right, width):
    over_row, aim = Regular(("row",), False), ColToRow(False)
    vmem = pl.BlockSpec(memory_space=pltpu.VMEM)
    slots = [over_row.slots(left), aim.slots(right)]
    shape = (width, left.shape[1] // width, right.shape[2] // width)
    return pl.pallas_call(
        functools.partial(triangle_kernel, width),
        out_shape=jax.ShapeDtypeStruct(shape, jnp.bfloat16),
        in_specs=[vmem] * 2,
        out_specs=vmem,
        scratch_shapes=[pltpu.VMEM(x.shape, x.dtype) for x in slots]
        + over_row.semaphores()
        + aim.semaphores(),
        compiler_params=pltpu.CompilerParams(
            collective_id=collective_id, has_side_effects=True, vmem_limit_bytes=48 << 20
        ),
    )(left, right)


def align_unfused(
    alignment, pair_normed, w_row, row_output_weight, w_bias, w_column, column_output_weight,
    outer_input_weight,
):
    rows = lax.axis_size("row")
    group_axes = ("branch", "row")
    groups_all = group_size(group_axes)
    seqs, residues, channels = alignment.shape
    tile_first, tile_second, _ = pair_normed.shape
    bias_tile = jnp.einsum(
        "ijc,ch->hij", pair_normed, w_bias, preferred_element_type=jnp.float32
    ).astype(jnp.bfloat16)
    row_normed = layer_norm(alignment).astype(jnp.bfloat16)
    bias_slots, row_slots = exchange(
        0,
        [Regular(("row",), False), Regular(("col",), False)],
        [bias_tile.reshape(HEAD_COUNT, -1), row_normed],
    )
    head_bias = jnp.transpose(
        bias_slots.reshape(rows, HEAD_COUNT, tile_first, tile_second), (1, 2, 0, 3)
    ).reshape(HEAD_COUNT, tile_first, rows * tile_second)
    local_weight = jnp.concatenate(
        [w_row[:, :ALIGN_CHANNELS], w_row[:, 3 * ALIGN_CHANNELS :]], axis=1
    )
    local_projected = project(row_normed, local_weight)
    query_matrix = (local_projected[..., :ALIGN_CHANNELS] * HEAD_CHANNELS ** (-0.5)).astype(
        jnp.bfloat16
    )
    gate_values = jax.nn.sigmoid(local_projected[..., ALIGN_CHANNELS:])
    gathered = jnp.transpose(row_slots, (1, 0, 2, 3)).reshape(seqs, -1, channels)
    key_value = project(gathered, w_row[:, ALIGN_CHANNELS : 3 * ALIGN_CHANNELS]).astype(
        jnp.bfloat16
    )
    key_matrix = key_value[..., :ALIGN_CHANNELS]
    value_matrix = key_value[..., ALIGN_CHANNELS:]
    attended = attend(query_matrix, key_matrix, value_matrix, head_bias, False)
    row_gated = (gate_values * attended).astype(jnp.bfloat16)
    alignment_row = (alignment.astype(jnp.float32) + project(row_gated, row_output_weight)).astype(
        jnp.bfloat16
    )
    part = residues // groups_all
    outgoing = jnp.transpose(
        alignment_row.reshape(seqs, groups_all, part, channels), (1, 0, 2, 3)
    ).reshape(groups_all, seqs * part, channels)
    (columns,) = exchange(1, [Regular(group_axes, True)], [outgoing])
    columns = columns.reshape(groups_all * seqs, part, channels)
    column_new = column_attention(columns, w_column, column_output_weight)
    outer_normed_input = layer_norm(column_new).astype(jnp.bfloat16)
    factor_pairs = project(outer_normed_input, outer_input_weight).astype(jnp.bfloat16)
    all_seqs = groups_all * seqs
    back, left_slots, right_slots = exchange(
        2,
        [Regular(group_axes, True), Regular(group_axes, False), ColToRow(True)],
        [
            column_new.reshape(groups_all, seqs * part, channels),
            factor_pairs[..., :FACTOR_CHANNELS].reshape(all_seqs, part * FACTOR_CHANNELS),
            factor_pairs[..., FACTOR_CHANNELS:].reshape(all_seqs, part * FACTOR_CHANNELS),
        ],
    )
    alignment_out = jnp.transpose(
        back.reshape(groups_all, seqs, part, channels), (1, 0, 2, 3)
    ).reshape(seqs, residues, channels)
    return alignment_out, left_slots, right_slots


def local(
    alignment,
    pair_features,
    w_row,
    row_output_weight,
    w_bias,
    w_column,
    column_output_weight,
    outer_input_weight,
    w_outer_out,
    w_triangle_in,
    w_triangle_gate,
    w_triangle_out,
):
    rows = lax.axis_size("row")
    group_axes = ("branch", "row")
    groups_all = group_size(group_axes)
    seqs, residues, channels = alignment.shape
    tile_first, tile_second, _ = pair_features.shape
    pair_normed = layer_norm(pair_features).astype(jnp.bfloat16)
    if (seqs * residues // groups_all) % 16 == 0 and residues % 16 == 0:
        bias = jnp.einsum(
            "ijc,ch->jhi", pair_normed, w_bias, preferred_element_type=jnp.float32
        ).astype(jnp.bfloat16)
        alignment_out, left_slots, right_slots = align_update(
            5,
            alignment,
            bias.reshape(tile_second, -1),
            w_row,
            row_output_weight,
            w_column,
            column_output_weight,
            outer_input_weight,
        )
    else:
        alignment_out, left_slots, right_slots = align_unfused(
            alignment,
            pair_normed,
            w_row,
            row_output_weight,
            w_bias,
            w_column,
            column_output_weight,
            outer_input_weight,
        )
    all_seqs = groups_all * seqs
    left_factor = jnp.transpose(left_slots, (1, 0, 2)).reshape(
        all_seqs, residues, FACTOR_CHANNELS
    )
    right_factor = jnp.transpose(right_slots, (1, 0, 2)).reshape(
        all_seqs, tile_second, FACTOR_CHANNELS
    )
    outer_update = outer_mean(left_factor, right_factor, w_outer_out)
    pair_mid = (pair_features.astype(jnp.float32) + outer_update.astype(jnp.float32)).astype(
        jnp.bfloat16
    )
    groups = lax.axis_size("branch")
    branch_width = TRIANGLE_WIDTH // groups
    branch_start = lax.axis_index("branch") * branch_width
    out_width = PAIR_WIDTH // groups
    out_start = lax.axis_index("branch") * out_width
    triangle_normed = layer_norm(pair_mid).astype(jnp.bfloat16)
    flat_normed = triangle_normed.reshape(-1, PAIR_WIDTH)
    w_in = lax.dynamic_slice_in_dim(
        w_triangle_in.reshape(PAIR_WIDTH, 4, TRIANGLE_WIDTH), branch_start, branch_width, 2
    )
    gate_weight = lax.dynamic_slice_in_dim(w_triangle_gate, out_start, out_width, 1)
    tri = jnp.einsum(
        "ikf,fpc->pkci", triangle_normed, w_in, preferred_element_type=jnp.float32
    )
    tri_left = (jax.nn.sigmoid(tri[1]) * tri[0]).astype(jnp.bfloat16)
    tri_right = (jax.nn.sigmoid(tri[3]) * tri[2]).astype(jnp.bfloat16)
    output_gate = jax.nn.sigmoid(
        lax.dot_general(
            gate_weight, flat_normed, (((0,), (1,)), ((), ())), preferred_element_type=jnp.float32
        )
    )
    per = rows // lax.axis_size("col")
    right_parts = jnp.transpose(
        tri_right.reshape(tile_second, branch_width, per, tile_second), (2, 0, 1, 3)
    )
    product = triangle_product(
        3,
        tri_left.reshape(tile_second, -1),
        right_parts.reshape(per, tile_second, -1),
        branch_width,
    )
    sums = jnp.transpose(product.reshape(branch_width, groups, -1), (1, 0, 2))
    mixed = mix_channels(4, sums, w_triangle_out)
    mixed = jnp.transpose(mixed, (1, 0, 2)).reshape(out_width, -1)
    update = jnp.transpose(output_gate * mixed.astype(jnp.float32))
    pair_slice = lax.dynamic_slice_in_dim(pair_mid, out_start, out_width, 2).reshape(-1, out_width)
    pair_out = (pair_slice.astype(jnp.float32) + update).astype(jnp.bfloat16)
    return (alignment_out, pair_out.reshape(tile_first, tile_second, out_width))


def solution(mesh):
    in_specs = (
        P(("branch", "row"), "col", None),
        P("col", "row", None),
        P(),
        P(),
        P(),
        P(),
        P(),
        P(),
        P(),
        P(),
        P(),
        P(),
    )
    out_specs = (P(("branch", "row"), "col", None), P("col", "row", "branch"))
    return jax.shard_map(local, mesh=mesh, in_specs=in_specs, out_specs=out_specs, check_vma=False)
```

```python
import functools

import jax
import jax.numpy as jnp
import numpy as np
from jax import lax
from jax.experimental import pallas as pl
from jax.experimental.pallas import tpu as pltpu
from jax.sharding import PartitionSpec as P

ALIGN_CHANNELS = 256
PAIR_WIDTH = 128
HEAD_COUNT = 8
HEAD_CHANNELS = 32
FACTOR_CHANNELS = 32
TRIANGLE_WIDTH = 128


EPSILON = 1e-05


def layer_norm(inputs):
    inputs = inputs.astype(jnp.float32)
    average = jnp.mean(inputs, axis=-1, keepdims=True)
    variance = jnp.mean(jnp.square(inputs - average), axis=-1, keepdims=True)
    return (inputs - average) * lax.rsqrt(variance + EPSILON)


def project(normed_input, weight_matrix):
    flat_rows = normed_input.reshape(-1, normed_input.shape[-1])
    result = jnp.dot(flat_rows, weight_matrix, preferred_element_type=jnp.float32)
    return result.reshape(normed_input.shape[:-1] + (weight_matrix.shape[1],))


def split_heads(row_entries):
    return row_entries.reshape(row_entries.shape[:-1] + (HEAD_COUNT, HEAD_CHANNELS))


def attend(query_matrix, key_matrix, value_matrix, head_bias, seq_major):
    query_heads = split_heads(query_matrix)
    key_heads = split_heads(key_matrix)
    value_heads = split_heads(value_matrix)
    if seq_major:
        scores = jnp.einsum(
            "qbhd,kbhd->bhqk", query_heads, key_heads, preferred_element_type=jnp.float32
        )
    else:
        scores = jnp.einsum(
            "bqhd,bkhd->bhqk", query_heads, key_heads, preferred_element_type=jnp.float32
        )
    if head_bias is not None:
        scores = scores + head_bias.astype(jnp.float32)[None]
    attention = jax.nn.softmax(scores, axis=-1).astype(jnp.bfloat16)
    if seq_major:
        mixed_channels = jnp.einsum(
            "bhqk,kbhd->qbhd", attention, value_heads, preferred_element_type=jnp.float32
        )
    else:
        mixed_channels = jnp.einsum(
            "bhqk,bkhd->bqhd", attention, value_heads, preferred_element_type=jnp.float32
        )
    return mixed_channels.reshape(mixed_channels.shape[:2] + (ALIGN_CHANNELS,))


def column_attention(row_entries, weight_matrix, output_weight):
    normed_input = layer_norm(row_entries).astype(jnp.bfloat16)
    projected_input = project(normed_input, weight_matrix)
    query_matrix = (projected_input[..., :ALIGN_CHANNELS] * HEAD_CHANNELS ** (-0.5)).astype(
        jnp.bfloat16
    )
    key_matrix = projected_input[..., ALIGN_CHANNELS : 2 * ALIGN_CHANNELS].astype(jnp.bfloat16)
    value_matrix = projected_input[..., 2 * ALIGN_CHANNELS : 3 * ALIGN_CHANNELS].astype(
        jnp.bfloat16
    )
    gate_values = jax.nn.sigmoid(projected_input[..., 3 * ALIGN_CHANNELS :])
    attended = attend(query_matrix, key_matrix, value_matrix, None, True)
    gated_output = (gate_values * attended).astype(jnp.bfloat16)
    return (row_entries.astype(jnp.float32) + project(gated_output, output_weight)).astype(
        jnp.bfloat16
    )


def outer_mean(left_factor, right_factor, w_outer_out):
    seq_count = left_factor.shape[0]
    outer_sum = jnp.einsum(
        "sic,sje->ijce", left_factor, right_factor, preferred_element_type=jnp.float32
    ) * (1.0 / seq_count)
    flat_rows = outer_sum.reshape(-1, FACTOR_CHANNELS * FACTOR_CHANNELS).astype(jnp.bfloat16)
    residual_update = jnp.dot(flat_rows, w_outer_out, preferred_element_type=jnp.float32)
    return residual_update.reshape(outer_sum.shape[:2] + (PAIR_WIDTH,)).astype(jnp.bfloat16)

MESH = pl.DeviceIdType.MESH


def group_size(axes):
    size = 1
    for axis in axes:
        size *= lax.axis_size(axis)
    return size


def group_index(axes):
    index = 0
    for axis in axes:
        index = index * lax.axis_size(axis) + lax.axis_index(axis)
    return index


def group_device(axes, index):
    device = {}
    for axis in reversed(axes):
        size = lax.axis_size(axis)
        device[axis] = lax.rem(index, size)
        index = index // size
    return device


def each_peer(axes, action):
    size = group_size(axes)
    me = group_index(axes)

    def step(offset, carry):
        action(offset, lax.rem(me + offset, size), lax.rem(me + size - offset, size))
        return carry

    if size <= 16:
        for offset in range(1, size):
            step(offset, 0)
    else:
        lax.fori_loop(1, size, step, 0)


def greet(axes):
    barrier = pltpu.get_barrier_semaphore()
    each_peer(
        axes,
        lambda offset, to, source: pl.semaphore_signal(
            barrier, inc=1, device_id=group_device(axes, to), device_id_type=MESH
        ),
    )
    return group_size(axes) - 1


class Regular:
    def __init__(self, axes, scatter):
        self.axes, self.scatter = axes, scatter

    def semaphores(self):
        size = group_size(self.axes)
        return [pltpu.SemaphoreType.DMA((size,)), pltpu.SemaphoreType.DMA((size,))]

    def slots(self, x):
        return x if self.scatter else jax.ShapeDtypeStruct(
            (group_size(self.axes),) + x.shape, x.dtype
        )

    def greet(self):
        return greet(self.axes)

    def block(self, ref, index):
        return ref.at[index] if self.scatter else ref

    def copy(self, src, dst, sems, offset, to):
        return pltpu.make_async_remote_copy(
            src_ref=self.block(src, to),
            dst_ref=dst.at[group_index(self.axes)],
            send_sem=sems[0].at[offset],
            recv_sem=sems[1].at[offset],
            device_id=group_device(self.axes, to),
            device_id_type=MESH,
        )

    def own(self, src, dst, sems):
        me = group_index(self.axes)
        return pltpu.make_async_copy(self.block(src, me), dst.at[me], sems[1].at[0])

    def start(self, src, dst, sems):
        each_peer(
            self.axes,
            lambda offset, to, source: self.copy(src, dst, sems, offset, to).start(),
        )
        self.own(src, dst, sems).start()

    def wait(self, src, dst, sems):
        self.own(src, dst, sems).wait()

        def finish(offset, to, source):
            arriving = pltpu.make_async_remote_copy(
                src_ref=self.block(src, to),
                dst_ref=dst.at[source],
                send_sem=sems[0].at[offset],
                recv_sem=sems[1].at[offset],
                device_id=group_device(self.axes, to),
                device_id_type=MESH,
            )
            arriving.wait_send()
            arriving.wait_recv()

        each_peer(self.axes, finish)


class ColToRow:
    def __init__(self, split):
        self.split = split

    def sizes(self):
        rows, cols = lax.axis_size("row"), lax.axis_size("col")
        return rows, cols, rows // cols

    def sends(self):
        rows, cols, per = self.sizes()
        return lax.axis_size("branch") * cols if self.split else per * cols

    def receives(self):
        rows, cols, per = self.sizes()
        return lax.axis_size("branch") * rows // per if self.split else rows

    def semaphores(self):
        return [
            pltpu.SemaphoreType.DMA((self.sends(),)),
            pltpu.SemaphoreType.DMA((self.receives(),)),
            pltpu.SemaphoreType.DMA((1,)),
        ]

    def slots(self, x):
        shape = x.shape if self.split else x.shape[1:]
        return jax.ShapeDtypeStruct((self.receives(),) + shape, x.dtype)

    def target(self, k):
        rows, cols, per = self.sizes()
        branch, row, col = (lax.axis_index(a) for a in ("branch", "row", "col"))
        if self.split:
            group = branch * rows + row
            part = lax.axis_size("branch") * rows // per
            return k // cols, col * per + group // part, k % cols
        return branch, col * per + k // cols, k % cols

    def slot(self):
        rows, cols, per = self.sizes()
        if self.split:
            group = lax.axis_index("branch") * rows + lax.axis_index("row")
            return lax.rem(group, lax.axis_size("branch") * rows // per)
        return lax.axis_index("row")

    def origin(self, k):
        rows, cols, per = self.sizes()
        row = lax.axis_index("row")
        if self.split:
            part = lax.axis_size("branch") * rows // per
            group = lax.rem(row, per) * part + k
            return group // rows, lax.rem(group, rows), row // per
        return lax.axis_index("branch"), k, row // per

    def mine(self, device):
        same = device[0] == lax.axis_index("branch")
        same = jnp.logical_and(same, device[1] == lax.axis_index("row"))
        return jnp.logical_and(same, device[2] == lax.axis_index("col"))

    def loop(self, count, body):
        if count <= 16:
            for k in range(count):
                body(k)
        else:
            lax.fori_loop(0, count, lambda k, carry: (body(k), carry)[1], 0)

    def each(self, count, device_of, away, here=None):
        def body(k):
            device = device_of(k)
            mine = self.mine(device)
            pl.when(jnp.logical_not(mine))(lambda: away(k, device))
            if here is not None:
                pl.when(mine)(lambda: here(k))

        self.loop(count, body)

    def greet(self):
        barrier = pltpu.get_barrier_semaphore()

        def signal(k, device):
            pl.semaphore_signal(barrier, inc=1, device_id=device, device_id_type=MESH)

        self.each(self.sends(), self.target, signal)
        self.each(self.receives(), self.origin, signal)
        rows, cols, per = self.sizes()
        row = lax.axis_index("row")
        if self.split:
            part = lax.axis_size("branch") * rows // per
            aimed = lax.axis_index("col") * per + group_index(("branch", "row")) // part
            mine = (aimed == row).astype(jnp.int32)
        else:
            mine = (row // per == lax.axis_index("col")).astype(jnp.int32)
        return self.sends() + self.receives() - 2 * mine

    def block(self, src, k):
        if self.split:
            return src
        return src.at[k // self.sizes()[1]]

    def start(self, src, dst, sems):
        def away(k, device):
            pltpu.make_async_remote_copy(
                src_ref=self.block(src, k),
                dst_ref=dst.at[self.slot()],
                send_sem=sems[0].at[k],
                recv_sem=sems[1].at[self.slot()],
                device_id=device,
                device_id_type=MESH,
            ).start()

        def here(k):
            pltpu.make_async_copy(self.block(src, k), dst.at[self.slot()], sems[2].at[0]).start()

        self.each(self.sends(), self.target, away, here)

    def wait(self, src, dst, sems):
        def sent(k, device):
            pltpu.make_async_remote_copy(
                src_ref=self.block(src, k),
                dst_ref=dst.at[self.slot()],
                send_sem=sems[0].at[k],
                recv_sem=sems[1].at[self.slot()],
                device_id=device,
                device_id_type=MESH,
            ).wait_send()

        def here(k):
            pltpu.make_async_copy(self.block(src, k), dst.at[self.slot()], sems[2].at[0]).wait()

        def arrived(k, device):
            pltpu.make_async_remote_copy(
                src_ref=self.block(src, 0),
                dst_ref=dst.at[k],
                send_sem=sems[0].at[0],
                recv_sem=sems[1].at[k],
                device_id=device,
                device_id_type=MESH,
            ).wait_recv()

        self.each(self.sends(), self.target, sent, here)
        self.each(self.receives(), self.origin, arrived)


def exchange_kernel(moves, *refs):
    count = len(moves)
    sources, slots, rest = refs[:count], refs[count : 2 * count], list(refs[2 * count :])
    sems = []
    for move in moves:
        width = len(move.semaphores())
        sems.append(rest[:width])
        rest = rest[width:]
    total = 0
    for move in moves:
        total += move.greet()
    pl.semaphore_wait(pltpu.get_barrier_semaphore(), total)
    for move, source, slot, sem in zip(moves, sources, slots, sems):
        move.start(source, slot, sem)
    for move, source, slot, sem in zip(moves, sources, slots, sems):
        move.wait(source, slot, sem)


def exchange(collective_id, moves, arrays):
    scratch = []
    for move in moves:
        scratch += move.semaphores()
    slots = [move.slots(x) for move, x in zip(moves, arrays)]
    any_space = pl.BlockSpec(memory_space=pl.ANY)
    return pl.pallas_call(
        functools.partial(exchange_kernel, moves),
        out_shape=[jax.ShapeDtypeStruct(s.shape, s.dtype) for s in slots],
        in_specs=[any_space] * len(moves),
        out_specs=[any_space] * len(moves),
        scratch_shapes=scratch,
        compiler_params=pltpu.CompilerParams(
            collective_id=collective_id, has_side_effects=True
        ),
    )(*arrays)


def mix_kernel(sums_ref, weight_ref, out_ref, held, mixed, *sems):
    move = Regular(("branch",), True)
    pl.semaphore_wait(pltpu.get_barrier_semaphore(), move.greet())
    move.start(sums_ref, held, sems[:2])
    move.wait(sums_ref, held, sems[:2])
    sums = held[...].astype(jnp.float32).reshape(-1, held.shape[-1])
    average = jnp.mean(sums, axis=0, keepdims=True)
    centred = sums - average
    variance = jnp.mean(jnp.square(centred), axis=0, keepdims=True)
    scaled = (centred * lax.rsqrt(variance + EPSILON)).astype(jnp.bfloat16)
    product = lax.dot_general(
        weight_ref[...], scaled, (((0,), (0,)), ((), ())), preferred_element_type=jnp.float32
    )
    mixed[...] = product.reshape(mixed.shape).astype(mixed.dtype)
    move.start(mixed, out_ref, sems[2:])
    move.wait(mixed, out_ref, sems[2:])


def mix_channels(collective_id, sums, weight):
    move = Regular(("branch",), True)
    groups, _, width = sums.shape
    out = jax.ShapeDtypeStruct((groups, weight.shape[1] // groups, width), jnp.bfloat16)
    vmem = pl.BlockSpec(memory_space=pltpu.VMEM)
    return pl.pallas_call(
        mix_kernel,
        out_shape=out,
        in_specs=[vmem, vmem],
        out_specs=vmem,
        scratch_shapes=[
            pltpu.VMEM(sums.shape, sums.dtype),
            pltpu.VMEM(out.shape, out.dtype),
        ]
        + move.semaphores()
        + move.semaphores(),
        compiler_params=pltpu.CompilerParams(
            collective_id=collective_id, has_side_effects=True, vmem_limit_bytes=32 << 20
        ),
    )(sums, weight)


def softmax_down(scores):
    peak = jnp.max(scores, axis=0, keepdims=True)
    powers = jnp.exp(scores - peak)
    return (powers / jnp.sum(powers, axis=0, keepdims=True)).astype(jnp.bfloat16)


def dot(a, b, a_dim=1, b_dim=0):
    return lax.dot_general(
        a, b, (((a_dim,), (b_dim,)), ((), ())), preferred_element_type=jnp.float32
    )


def align_kernel(
    seqs,
    part,
    align_ref,
    bias_ref,
    w_row_far,
    row_out_far,
    w_col_far,
    col_out_far,
    w_left_far,
    w_right_far,
    permute_far,
    same_far,
    out_ref,
    left_slots,
    right_slots,
    normed,
    bias_slots,
    gathered,
    outgoing,
    columns,
    col_new,
    back,
    normed_cols,
    left,
    right,
    w_row_ref,
    row_out_ref,
    w_col_ref,
    col_out_ref,
    w_left_ref,
    w_right_ref,
    permute_ref,
    same_ref,
    weight_sems,
    *sems,
):
    fetches = [
        pltpu.make_async_copy(far, near, weight_sems.at[n])
        for n, (far, near) in enumerate(
            (
                (w_row_far, w_row_ref),
                (row_out_far, row_out_ref),
                (permute_far, permute_ref),
                (w_col_far, w_col_ref),
                (col_out_far, col_out_ref),
                (w_left_far, w_left_ref),
                (w_right_far, w_right_ref),
                (same_far, same_ref),
            )
        )
    ]
    for fetch in fetches:
        fetch.start()
    bf16, width = jnp.bfloat16, ALIGN_CHANNELS
    group_axes = ("branch", "row")
    groups = group_size(group_axes)
    over_row, over_col = Regular(("row",), False), Regular(("col",), False)
    swap, spread, aim = Regular(group_axes, True), Regular(group_axes, False), ColToRow(True)
    total = swap.greet() + over_col.greet() + aim.greet()
    pl.semaphore_wait(pltpu.get_barrier_semaphore(), total)
    over_row.start(bias_ref, bias_slots, sems[0:2])
    normed[...] = layer_norm(align_ref[...]).astype(bf16)
    over_col.start(normed, gathered, sems[2:4])
    residues = align_ref.shape[0] // seqs
    fetches[0].wait()
    lanes = lax.broadcasted_iota(jnp.int32, (residues, width), 1)
    picks = [
        (lanes >= h * HEAD_CHANNELS) & (lanes < (h + 1) * HEAD_CHANNELS) for h in range(HEAD_COUNT)
    ]
    query = dot(normed[...], w_row_ref[:, :width]) * HEAD_CHANNELS ** (-0.5)
    gate = jax.nn.sigmoid(dot(normed[...], w_row_ref[:, 3 * width :]))
    over_col.wait(normed, gathered, sems[2:4])
    cols = gathered.shape[0]
    key_value = [
        dot(gathered[q], w_row_ref[:, width : 3 * width]).astype(bf16) for q in range(cols)
    ]
    over_row.wait(bias_ref, bias_slots, sems[0:2])
    bias = bias_slots[...].astype(jnp.float32).reshape(-1, bias_ref.shape[1])
    mixed = []
    for s in range(seqs):
        own = slice(s * residues, (s + 1) * residues)
        key = jnp.concatenate([kv[own, :width] for kv in key_value], axis=0)
        value = jnp.concatenate([kv[own, width:] for kv in key_value], axis=0)
        heads = jnp.concatenate([jnp.where(p, query[own], 0.0) for p in picks], axis=0)
        weights = softmax_down(dot(key, heads.astype(bf16), 1, 1) + bias)
        spreadout = dot(weights, value, 0, 0)
        attended = jnp.zeros((residues, width), jnp.float32)
        for h, p in enumerate(picks):
            attended = jnp.where(p, spreadout[h * residues : (h + 1) * residues], attended)
        mixed.append(attended)
    row_gated = (gate * jnp.concatenate(mixed, axis=0)).astype(bf16)
    fetches[1].wait()
    fetches[2].wait()
    updated = align_ref[...].astype(jnp.float32) + dot(row_gated, row_out_ref[...])
    outgoing[...] = dot(permute_ref[...], updated.astype(bf16)).astype(bf16).reshape(outgoing.shape)
    swap.start(outgoing, columns, sems[4:6])
    for fetch in fetches[3:]:
        fetch.wait()
    swap.wait(outgoing, columns, sems[4:6])
    entries = columns[...].reshape(-1, width)
    count = entries.shape[0]
    col_normed = layer_norm(entries).astype(bf16)
    projected = dot(col_normed, w_col_ref[...])
    query = projected[:, :width] * HEAD_CHANNELS ** (-0.5)
    key = projected[:, width : 2 * width].astype(bf16)
    value = projected[:, 2 * width : 3 * width].astype(bf16)
    gate = jax.nn.sigmoid(projected[:, 3 * width :])
    same = same_ref[...].astype(jnp.float32) > 0.5
    lanes = lax.broadcasted_iota(jnp.int32, (count, width), 1)
    attended = jnp.zeros((count, width), jnp.float32)
    for h in range(HEAD_COUNT):
        pick = (lanes >= h * HEAD_CHANNELS) & (lanes < (h + 1) * HEAD_CHANNELS)
        scores = dot(key, jnp.where(pick, query, 0.0).astype(bf16), 1, 1)
        weights = softmax_down(jnp.where(same, scores, jnp.finfo(jnp.float32).min))
        attended = jnp.where(pick, dot(weights, value, 0, 0), attended)
    col_gated = (gate * attended).astype(bf16)
    new = (entries.astype(jnp.float32) + dot(col_gated, col_out_ref[...])).astype(bf16)
    normed_new = layer_norm(new)
    for half in range(width // 128):
        normed_cols[half] = normed_new[:, half * 128 : (half + 1) * 128]
    all_seqs = count // part
    left_sum = right_sum = None
    for r in range(part):
        rows_r = jnp.concatenate(
            [normed_cols[half, pl.ds(r, all_seqs, stride=part), :] for half in range(width // 128)],
            axis=1,
        ).astype(bf16)
        left_r, right_r = dot(rows_r, w_left_ref[r]), dot(rows_r, w_right_ref[r])
        left_sum = left_r if r == 0 else left_sum + left_r
        right_sum = right_r if r == 0 else right_sum + right_r
    left[...] = left_sum.astype(bf16)
    right[...] = right_sum.astype(bf16)
    aim.start(right, right_slots, sems[10:13])
    spread.start(left, left_slots, sems[8:10])
    col_new[...] = new.reshape(col_new.shape)
    swap.start(col_new, back, sems[6:8])
    swap.wait(col_new, back, sems[6:8])
    result = dot(permute_ref[...], back[...].reshape(-1, width), 0, 0)
    out_ref[...] = result.astype(bf16)
    aim.wait(right, right_slots, sems[10:13])
    spread.wait(left, left_slots, sems[8:10])


def align_update(collective_id, alignment, bias, w_row, row_out, w_col, col_out, w_factor):
    bf16 = jnp.bfloat16
    seqs, residues, width = alignment.shape
    group_axes = ("branch", "row")
    groups = group_size(group_axes)
    part = residues // groups
    count = seqs * residues
    place = np.arange(count).reshape(seqs, groups, part).transpose(1, 0, 2).reshape(-1)
    permute = jnp.asarray(np.eye(count, dtype=np.float32)[place], bf16)
    rest = np.arange(count) % part
    same = jnp.asarray((rest[:, None] == rest[None, :]).astype(np.float32), bf16)
    eye = jnp.asarray(np.eye(part, dtype=np.float32), bf16)
    spread_out = lambda w: (eye[:, None, :, None] * w[None, :, None, :]).reshape(part, width, -1)
    w_left = spread_out(w_factor[:, :FACTOR_CHANNELS])
    w_right = spread_out(w_factor[:, FACTOR_CHANNELS:])
    over_row, over_col = Regular(("row",), False), Regular(("col",), False)
    swap, spread, aim = Regular(group_axes, True), Regular(group_axes, False), ColToRow(True)
    factor = jax.ShapeDtypeStruct((groups * seqs, part * FACTOR_CHANNELS), bf16)
    slots = (groups, seqs * part, width)
    scratch = [
        pltpu.VMEM((count, width), bf16),
        pltpu.VMEM((lax.axis_size("row"),) + bias.shape, bf16),
        pltpu.VMEM((lax.axis_size("col"), count, width), bf16),
        pltpu.VMEM(slots, bf16),
        pltpu.VMEM(slots, bf16),
        pltpu.VMEM(slots, bf16),
        pltpu.VMEM(slots, bf16),
        pltpu.VMEM((width // 128, count, 128), jnp.float32),
        pltpu.VMEM(factor.shape, bf16),
        pltpu.VMEM(factor.shape, bf16),
    ]
    weights = (w_row, row_out, w_col, col_out, w_left, w_right, permute, same)
    scratch += [pltpu.VMEM(w.shape, w.dtype) for w in weights]
    scratch += [pltpu.SemaphoreType.DMA((len(weights),))]
    for move in (over_row, over_col, swap, swap, spread, aim):
        scratch += move.semaphores()
    vmem = pl.BlockSpec(memory_space=pltpu.VMEM)
    anywhere = pl.BlockSpec(memory_space=pl.ANY)
    far = pl.BlockSpec(memory_space=pltpu.MemorySpace.HBM)
    out, left_slots, right_slots = pl.pallas_call(
        functools.partial(align_kernel, seqs, part),
        out_shape=[
            jax.ShapeDtypeStruct((count, width), bf16),
            spread.slots(factor),
            aim.slots(factor),
        ],
        in_specs=[vmem] * 2 + [far] * 8,
        out_specs=[vmem, anywhere, anywhere],
        scratch_shapes=scratch,
        compiler_params=pltpu.CompilerParams(
            collective_id=collective_id, has_side_effects=True, vmem_limit_bytes=60 << 20
        ),
    )(
        alignment.reshape(count, width),
        bias,
        *weights,
    )
    return out.reshape(alignment.shape), left_slots, right_slots


def triangle_kernel(width, left_ref, right_ref, out_ref, left_slots, right_slots, *sems):
    over_row, aim = Regular(("row",), False), ColToRow(False)
    total = over_row.greet() + aim.greet()
    pl.semaphore_wait(pltpu.get_barrier_semaphore(), total)
    over_row.start(left_ref, left_slots, sems[0:2])
    aim.start(right_ref, right_slots, sems[2:5])
    over_row.wait(left_ref, left_slots, sems[0:2])
    aim.wait(right_ref, right_slots, sems[2:5])
    left = left_slots[...].reshape(-1, left_ref.shape[-1])
    right = right_slots[...].reshape(-1, right_ref.shape[-1])
    first, second = left.shape[1] // width, right.shape[1] // width
    batch = max(1, 128 // min(first, second))
    for start in range(0, width, batch):
        product = dot(
            left[:, start * first : (start + batch) * first],
            right[:, start * second : (start + batch) * second],
            0,
            0,
        )
        for c in range(batch):
            out_ref[start + c] = product[
                c * first : (c + 1) * first, c * second : (c + 1) * second
            ].astype(out_ref.dtype)


def triangle_product(collective_id, left, right, width):
    over_row, aim = Regular(("row",), False), ColToRow(False)
    vmem = pl.BlockSpec(memory_space=pltpu.VMEM)
    slots = [over_row.slots(left), aim.slots(right)]
    shape = (width, left.shape[1] // width, right.shape[2] // width)
    return pl.pallas_call(
        functools.partial(triangle_kernel, width),
        out_shape=jax.ShapeDtypeStruct(shape, jnp.bfloat16),
        in_specs=[vmem] * 2,
        out_specs=vmem,
        scratch_shapes=[pltpu.VMEM(x.shape, x.dtype) for x in slots]
        + over_row.semaphores()
        + aim.semaphores(),
        compiler_params=pltpu.CompilerParams(
            collective_id=collective_id, has_side_effects=True, vmem_limit_bytes=48 << 20
        ),
    )(left, right)


def align_unfused(
    alignment, pair_normed, w_row, row_output_weight, w_bias, w_column, column_output_weight,
    outer_input_weight,
):
    rows = lax.axis_size("row")
    group_axes = ("branch", "row")
    groups_all = group_size(group_axes)
    seqs, residues, channels = alignment.shape
    tile_first, tile_second, _ = pair_normed.shape
    bias_tile = jnp.einsum(
        "ijc,ch->hij", pair_normed, w_bias, preferred_element_type=jnp.float32
    ).astype(jnp.bfloat16)
    row_normed = layer_norm(alignment).astype(jnp.bfloat16)
    bias_slots, row_slots = exchange(
        0,
        [Regular(("row",), False), Regular(("col",), False)],
        [bias_tile.reshape(HEAD_COUNT, -1), row_normed],
    )
    head_bias = jnp.transpose(
        bias_slots.reshape(rows, HEAD_COUNT, tile_first, tile_second), (1, 2, 0, 3)
    ).reshape(HEAD_COUNT, tile_first, rows * tile_second)
    local_weight = jnp.concatenate(
        [w_row[:, :ALIGN_CHANNELS], w_row[:, 3 * ALIGN_CHANNELS :]], axis=1
    )
    local_projected = project(row_normed, local_weight)
    query_matrix = (local_projected[..., :ALIGN_CHANNELS] * HEAD_CHANNELS ** (-0.5)).astype(
        jnp.bfloat16
    )
    gate_values = jax.nn.sigmoid(local_projected[..., ALIGN_CHANNELS:])
    gathered = jnp.transpose(row_slots, (1, 0, 2, 3)).reshape(seqs, -1, channels)
    key_value = project(gathered, w_row[:, ALIGN_CHANNELS : 3 * ALIGN_CHANNELS]).astype(
        jnp.bfloat16
    )
    key_matrix = key_value[..., :ALIGN_CHANNELS]
    value_matrix = key_value[..., ALIGN_CHANNELS:]
    attended = attend(query_matrix, key_matrix, value_matrix, head_bias, False)
    row_gated = (gate_values * attended).astype(jnp.bfloat16)
    alignment_row = (alignment.astype(jnp.float32) + project(row_gated, row_output_weight)).astype(
        jnp.bfloat16
    )
    part = residues // groups_all
    outgoing = jnp.transpose(
        alignment_row.reshape(seqs, groups_all, part, channels), (1, 0, 2, 3)
    ).reshape(groups_all, seqs * part, channels)
    (columns,) = exchange(1, [Regular(group_axes, True)], [outgoing])
    columns = columns.reshape(groups_all * seqs, part, channels)
    column_new = column_attention(columns, w_column, column_output_weight)
    outer_normed_input = layer_norm(column_new).astype(jnp.bfloat16)
    factor_pairs = project(outer_normed_input, outer_input_weight).astype(jnp.bfloat16)
    all_seqs = groups_all * seqs
    back, left_slots, right_slots = exchange(
        2,
        [Regular(group_axes, True), Regular(group_axes, False), ColToRow(True)],
        [
            column_new.reshape(groups_all, seqs * part, channels),
            factor_pairs[..., :FACTOR_CHANNELS].reshape(all_seqs, part * FACTOR_CHANNELS),
            factor_pairs[..., FACTOR_CHANNELS:].reshape(all_seqs, part * FACTOR_CHANNELS),
        ],
    )
    alignment_out = jnp.transpose(
        back.reshape(groups_all, seqs, part, channels), (1, 0, 2, 3)
    ).reshape(seqs, residues, channels)
    return alignment_out, left_slots, right_slots


def local(
    alignment,
    pair_features,
    w_row,
    row_output_weight,
    w_bias,
    w_column,
    column_output_weight,
    outer_input_weight,
    w_outer_out,
    w_triangle_in,
    w_triangle_gate,
    w_triangle_out,
):
    rows = lax.axis_size("row")
    group_axes = ("branch", "row")
    groups_all = group_size(group_axes)
    seqs, residues, channels = alignment.shape
    tile_first, tile_second, _ = pair_features.shape
    pair_normed = layer_norm(pair_features).astype(jnp.bfloat16)
    if (seqs * residues // groups_all) % 16 == 0 and residues % 16 == 0:
        bias = jnp.einsum(
            "ijc,ch->jhi", pair_normed, w_bias, preferred_element_type=jnp.float32
        ).astype(jnp.bfloat16)
        alignment_out, left_slots, right_slots = align_update(
            5,
            alignment,
            bias.reshape(tile_second, -1),
            w_row,
            row_output_weight,
            w_column,
            column_output_weight,
            outer_input_weight,
        )
    else:
        alignment_out, left_slots, right_slots = align_unfused(
            alignment,
            pair_normed,
            w_row,
            row_output_weight,
            w_bias,
            w_column,
            column_output_weight,
            outer_input_weight,
        )
    all_seqs = groups_all * seqs
    left_factor = jnp.transpose(left_slots, (1, 0, 2)).reshape(
        all_seqs, residues, FACTOR_CHANNELS
    )
    right_factor = jnp.transpose(right_slots, (1, 0, 2)).reshape(
        all_seqs, tile_second, FACTOR_CHANNELS
    )
    outer_update = outer_mean(left_factor, right_factor, w_outer_out)
    pair_mid = (pair_features.astype(jnp.float32) + outer_update.astype(jnp.float32)).astype(
        jnp.bfloat16
    )
    groups = lax.axis_size("branch")
    branch_width = TRIANGLE_WIDTH // groups
    branch_start = lax.axis_index("branch") * branch_width
    out_width = PAIR_WIDTH // groups
    out_start = lax.axis_index("branch") * out_width
    triangle_normed = layer_norm(pair_mid).astype(jnp.bfloat16)
    flat_normed = triangle_normed.reshape(-1, PAIR_WIDTH)
    w_in = lax.dynamic_slice_in_dim(
        w_triangle_in.reshape(PAIR_WIDTH, 4, TRIANGLE_WIDTH), branch_start, branch_width, 2
    )
    gate_weight = lax.dynamic_slice_in_dim(w_triangle_gate, out_start, out_width, 1)
    tri = jnp.einsum(
        "ikf,fpc->pkci", triangle_normed, w_in, preferred_element_type=jnp.float32
    )
    tri_left = (jax.nn.sigmoid(tri[1]) * tri[0]).astype(jnp.bfloat16)
    tri_right = (jax.nn.sigmoid(tri[3]) * tri[2]).astype(jnp.bfloat16)
    output_gate = jax.nn.sigmoid(
        lax.dot_general(
            gate_weight, flat_normed, (((0,), (1,)), ((), ())), preferred_element_type=jnp.float32
        )
    )
    per = rows // lax.axis_size("col")
    right_parts = jnp.transpose(
        tri_right.reshape(tile_second, branch_width, per, tile_second), (2, 0, 1, 3)
    )
    product = triangle_product(
        3,
        tri_left.reshape(tile_second, -1),
        right_parts.reshape(per, tile_second, -1),
        branch_width,
    )
    sums = jnp.transpose(product.reshape(branch_width, groups, -1), (1, 0, 2))
    mixed = mix_channels(4, sums, w_triangle_out)
    mixed = jnp.transpose(mixed, (1, 0, 2)).reshape(out_width, -1)
    update = jnp.transpose(output_gate * mixed.astype(jnp.float32))
    pair_slice = lax.dynamic_slice_in_dim(pair_mid, out_start, out_width, 2).reshape(-1, out_width)
    pair_out = (pair_slice.astype(jnp.float32) + update).astype(jnp.bfloat16)
    return (alignment_out, pair_out.reshape(tile_first, tile_second, out_width))


def solution(mesh):
    in_specs = (
        P(("branch", "row"), "col", None),
        P("col", "row", None),
        P(),
        P(),
        P(),
        P(),
        P(),
        P(),
        P(),
        P(),
        P(),
        P(),
    )
    out_specs = (P(("branch", "row"), "col", None), P("col", "row", "branch"))
    return jax.shard_map(local, mesh=mesh, in_specs=in_specs, out_specs=out_specs, check_vma=False)
```
